128 devices in a mesh: dp: 32 (over z, y, core), expert: 2 (over x_hi), tensor: 2 (over x_lo).
Axes of the slice: x: 4 (x_hi: 2, x_lo: 2; x = x_hi * 2 + x_lo), y: 4, z: 4, core: 2. Of those that a mesh axis runs over, the one named last changes fastest.
Arguments:
- tokens: bfloat16 [2048, 4096], P('dp', 'tensor'), may hold values from -6 to 6
- targets: bfloat16 [2048, 4096], P('dp', 'tensor'), may hold values from -6 to 6
- norm_gain: float32 [4096], P('tensor'), may hold values from 0.1 to 1.9
- expert_ids: int32 [2048, 2], P('dp'), may hold values from 0 to 7, all different within a row; in each aligned block of 64 rows (0 to 63, 64 to 127, ...) at most 18 rows name the same one
- gate_prob: float32 [2048, 2], P('dp'), may hold values from 0.2 to 1
- w_gate: bfloat16 [4096, 65536], P('tensor', ('dp', 'expert')), may hold values from -0.09375 to 0.09375
- gate_probe: bfloat16 [4096, 65536], P('tensor', ('dp', 'expert')), as said below
- w_up: bfloat16 [4096, 65536], P('tensor', ('dp', 'expert')), may hold values from -0.09375 to 0.09375
- w_down: bfloat16 [65536, 4096], P(('dp', 'expert'), 'tensor'), may hold values from -0.0625 to 0.0625
Outputs:
- normed: bfloat16 [2048, 4096], P('dp', 'tensor')
- curvature: float32 [2048, 2], P('dp')
- estimate: float32 [8], replicated
The draws below stay inside these ranges and needn't reach their ends.
Inputs may be any that keep to these rules, and one draw needn't show every extreme that they name: `expert_ids`: the two ids of a token differ; within each block of 64 consecutive tokens no expert is named more than 18 times; every expert is named by some token. `gate_probe`: every entry is plus or minus 1 / sqrt(4096).
All inputs are finite; a program needn't handle non-finite values.
Results may differ from the reference program's by a relative error of at most 0.03.
Values may be sent and summed in bfloat16 or wider, within the bound.
A program may use at most 128 MiB of HBM per device.

```python
import math
import jax
import jax.numpy as jnp
import numpy as np
from jax import lax

D = 4096
FF = 8192
EXPERTS = 8
TOK_DEV = 64
CAP = 18
TOKENS = 2048
N_DP = 32
N_EXPERT = 2
N_TENSOR = 2


def draw_gate_probe(key, part):
    signs = jax.random.bernoulli(key, 0.5, (D, EXPERTS * FF))
    values = jnp.where(signs, 1.0, -1.0).astype(jnp.float32) * D ** (-0.5)
    return values.astype(jnp.bfloat16)


def block_levels(own_key, extent, cuts, low, largest):
    factor_of = 1.0
    for position, parts in cuts:
        heights = jax.random.uniform(jax.random.fold_in(jax.random.fold_in(own_key, 6), position), (parts,), jnp.float32, low / len(cuts), largest / len(cuts))
        factor_of = factor_of * jnp.repeat(jnp.exp(heights), extent[position] // parts).reshape((-1,) + (1,) * (len(extent) - 1 - position))
    return factor_of


def deal_out(key, own, number, rows, amount, top, bound, lean):
    sequence = jax.random.permutation(key, amount)
    packed, common = load_shares(amount, rows * top, bound, lean, True), load_shares(amount, rows * top, bound, lean, False)
    places = jnp.arange(amount)

    def named(lengths, rotation):
        used = int((lengths > 0).sum())
        fixed = max(1, used // 4)
        passed = fixed + (places - fixed + rotation * (used - fixed)) % max(1, amount - fixed)
        return jnp.zeros((amount,), jnp.int32).at[sequence[jnp.where(places < fixed, places, passed)]].set(jnp.asarray(lengths, jnp.int32))

    lengths = jnp.where(number % 4 == 0, named(packed, number // 4), named(common, number - number // 4 - 1))
    mixed = jax.random.permutation(jax.random.fold_in(own, 3), amount)
    donor, taker = mixed[0:amount // 2 * 2:2], mixed[1:amount // 2 * 2:2]
    margin = jnp.minimum(lengths[donor] - 1, bound - lengths[taker]) // 2
    margin = jnp.where((donor == sequence[0]) | (taker == sequence[0]) | (lengths[taker] == 0), 0, jnp.maximum(margin, 0))
    passed = jax.random.randint(jax.random.fold_in(own, 4), (amount // 2,), 0, 1 << 20) % (margin + 1)
    lengths = lengths.at[donor].add(-passed).at[taker].add(passed)
    items = jnp.searchsorted(jnp.cumsum(lengths), jnp.arange(rows * top), side="right").astype(jnp.int32)
    listing = items.reshape(top, rows).T
    listing = listing[jax.random.permutation(jax.random.fold_in(own, 1), rows)]
    rotation = jax.random.randint(jax.random.fold_in(own, 2), (rows, 1), 0, top)
    return jnp.take_along_axis(listing, (jnp.arange(top)[None, :] + rotation) % top, axis=1)


def load_shares(number_of, total, limit, lean, full):
    loads = [(1 << 20) // math.isqrt(grade ** lean) + 1 for grade in range(1, number_of + 1)]
    largest = limit if full else min(limit, max(-(-total // number_of), total * loads[0] // sum(loads)))
    least = 1 if total - largest >= number_of - 1 else 0
    given, rest = [largest] + [least] * (number_of - 1), total - largest - least * (number_of - 1)
    while rest > 0:
        free = [i for i in range(1, number_of) if given[i] < largest] or [i for i in range(1, number_of) if given[i] < limit]
        whole, left = sum([loads[i] for i in free]), rest
        for i in free:
            addition = min(limit - given[i], max(1, left * loads[i] // whole), rest)
            given[i] = given[i] + addition
            rest = rest - addition
    return np.array(given)


def gaussian(key, extent, scale, most, shards=(), kind=jnp.bfloat16):
    level = block_levels(key, extent, shards, -0.22, 0.18) if shards else 1.0
    drawn = jax.random.normal(key, extent, jnp.float32) * scale * level
    return jnp.minimum(jnp.maximum(drawn, -most), most).astype(kind)


def setup_inputs(seed: int = 0) -> dict:
    key_of = jax.random.split(jax.random.key(seed), 10)
    tokens = gaussian(key_of[0], (TOKENS, D), 1.0, 6.0, ((0, 32), (1, 2)))
    targets = gaussian(key_of[1], (TOKENS, D), 1.0, 6.0, ((0, 32), (1, 2)))
    norm_gain = jnp.clip(1.0 + 0.18 * jax.random.normal(key_of[2], (D,), jnp.float32), 0.1, 1.9)
    expert_ids_keys = jax.random.split(jax.random.fold_in(key_of[3], 1), TOKENS // TOK_DEV)
    expert_ids_turns = jax.random.permutation(jax.random.fold_in(key_of[3], 3), TOKENS // TOK_DEV)
    expert_ids = jax.vmap(lambda own, number: deal_out(jax.random.fold_in(key_of[3], 2), own, number, TOK_DEV, EXPERTS, 2, CAP, 2))(expert_ids_keys, expert_ids_turns).reshape((TOKENS, 2))
    gate_prob = jnp.clip(0.2 + 0.8 * jax.random.uniform(key_of[4], (TOKENS, 2), jnp.float32) ** block_levels(key_of[4], (TOKENS, 2), ((0, 32),), -0.2, 0.2), 0.2, 1.0)
    w_gate = gaussian(key_of[5], (D, EXPERTS * FF), D ** -0.5, 0.09375, ((0, 2), (1, 64)))
    gate_probe = draw_gate_probe(jax.random.fold_in(key_of[9], 71), 0)
    w_up = gaussian(key_of[7], (D, EXPERTS * FF), D ** -0.5, 0.09375, ((0, 2), (1, 64)))
    w_down = gaussian(key_of[8], (EXPERTS * FF, D), FF ** -0.5, 0.0625, ((0, 64), (1, 2)))
    return {"tokens": tokens, "targets": targets, "norm_gain": norm_gain, "expert_ids": expert_ids, "gate_prob": gate_prob, "w_gate": w_gate, "gate_probe": gate_probe, "w_up": w_up, "w_down": w_down}


epsilon = 1e-05
loss_weight = 8.0

def derivative_jets(preact):
    gate_in = preact[:, 0]
    gate_dir = preact[:, 1]
    up_in = preact[:, 2]
    sigmoid_in = jax.nn.sigmoid(gate_in)
    first_slope = sigmoid_in * (1.0 + gate_in * (1.0 - sigmoid_in))
    second_slope = sigmoid_in * (1.0 - sigmoid_in) * (2.0 + gate_in * (1.0 - 2.0 * sigmoid_in))
    primal = gate_in * sigmoid_in * up_in
    tangent = first_slope * gate_dir * up_in
    second = second_slope * gate_dir * gate_dir * up_in
    return jnp.stack([primal, tangent, second], axis=1).astype(jnp.bfloat16)

def slot_numbers(expert_ids):
    blocks = expert_ids.reshape(N_DP, TOK_DEV * 2)
    onehot = (blocks[:, :, None] == jnp.arange(EXPERTS, dtype=jnp.int32)).astype(jnp.int32)
    before = jnp.cumsum(onehot, axis=1).astype(jnp.int32) - onehot
    return lax.optimization_barrier(jnp.sum(before * onehot, axis=2)).astype(jnp.int32).reshape(TOKENS, 2)

def blocked_sum(left_blocks, right_blocks):
    partial_value = jnp.einsum('rbi,bic->rbc', left_blocks, right_blocks)
    rounded = lax.optimization_barrier(partial_value.astype(jnp.bfloat16))
    return lax.optimization_barrier(jnp.sum(rounded.astype(jnp.float32), axis=1))

def reference(tokens, targets, norm_gain, expert_ids, gate_prob, w_gate, gate_probe, w_up, w_down):
    slot_rows = N_DP * CAP
    width_part = D // N_TENSOR
    pieces = N_DP * N_EXPERT // EXPERTS
    hidden_part = FF // pieces
    slot_index = slot_numbers(expert_ids)
    owner_index = (jnp.arange(TOKENS, dtype=jnp.int32) // TOK_DEV).astype(jnp.int32)[:, None]
    places = ((expert_ids * N_DP + owner_index) * CAP + slot_index).reshape(-1).astype(jnp.int32)
    dispatched = jnp.zeros((EXPERTS * slot_rows, D), jnp.bfloat16).at[places].set(jnp.repeat(tokens, 2, axis=0))
    dispatched = dispatched.reshape(EXPERTS, slot_rows, D)

    def expert_images(carried):
        expert_index, expert_rows = carried
        split_rows = expert_rows.astype(jnp.float32).reshape(slot_rows, N_TENSOR, width_part)

        def preact_of(weight):
            weight_cols = lax.dynamic_slice_in_dim(weight, expert_index * FF, FF, 1)
            return blocked_sum(split_rows, weight_cols.astype(jnp.float32).reshape(N_TENSOR, width_part, FF))
        hidden_jets = derivative_jets(jnp.stack([preact_of(w_gate), preact_of(gate_probe), preact_of(w_up)], axis=1))
        down_rows = lax.dynamic_slice_in_dim(w_down, expert_index * FF, FF, 0)
        down_rows = down_rows.astype(jnp.float32).reshape(pieces, hidden_part, D)
        images = blocked_sum(hidden_jets.astype(jnp.float32).reshape(slot_rows * 3, pieces, hidden_part), down_rows)
        return images.reshape(slot_rows, 3, D)
    expert_table = lax.map(expert_images, (jnp.arange(EXPERTS, dtype=jnp.int32), dispatched))
    picked = expert_table.reshape(EXPERTS * slot_rows, 3, D)[places].reshape(TOKENS, 2, 3, D)
    weights = gate_prob[:, :, None]
    summed = tokens.astype(jnp.float32) + lax.optimization_barrier(jnp.sum(weights * picked[:, :, 0], axis=1))
    tangent_out = weights * picked[:, :, 1]
    second_out = weights * picked[:, :, 2]
    target = targets.astype(jnp.float32)
    inv_root = lax.rsqrt(lax.optimization_barrier(jnp.mean(summed * summed, axis=-1)) + epsilon)
    normed = (norm_gain * summed * inv_root[:, None]).astype(jnp.bfloat16)

    def slot_loss(travel):
        shifted = summed[:, None, :] + travel[:, :, None] * tangent_out + 0.5 * (travel * travel)[:, :, None] * second_out
        inv_scale = lax.rsqrt(lax.optimization_barrier(jnp.mean(shifted * shifted, axis=-1)) + epsilon)
        misfit = norm_gain * shifted * inv_scale[:, :, None] - target[:, None, :]
        return loss_weight / D * lax.optimization_barrier(jnp.sum(misfit * misfit, axis=-1))
    unit_step = jnp.ones((TOKENS, 2), jnp.float32)

    def slope_at(travel):
        return jax.jvp(slot_loss, (travel,), (unit_step,))[1]
    curvature = jax.jvp(slope_at, (jnp.zeros((TOKENS, 2), jnp.float32),), (unit_step,))[1]
    member = (expert_ids[:, :, None] == jnp.arange(EXPERTS, dtype=jnp.int32)).astype(jnp.float32)
    totals = lax.optimization_barrier(jnp.sum(member * curvature[:, :, None], axis=(0, 1)))
    counts = lax.optimization_barrier(jnp.sum(member, axis=(0, 1)))
    return (normed, curvature, totals / counts)
```

```python
import jax
import jax.numpy as jnp
from jax import lax
from jax.sharding import PartitionSpec as P

D = 4096
EXPERTS = 8
CAP = 18


epsilon = 1e-05
loss_weight = 8.0


def sent_to_all(x, axis):
    copies = jnp.broadcast_to(x, (lax.axis_size(axis), *x.shape))
    return lax.all_to_all(copies, axis, split_axis=0, concat_axis=0, tiled=True)


def of_everyone(x, axis):
    everything = sent_to_all(x, axis)
    return jnp.sum(everything.astype(jnp.float32), axis=0)


def of_everyone_2(x, axis):
    everything = sent_to_all(x, axis)
    return jnp.sum(everything, axis=0)


def packed_total(arrays, axis):
    ends = [0]
    for a in arrays:
        ends.append(ends[-1] + a.size)
    running = of_everyone_2(jnp.concatenate([a.ravel() for a in arrays]), axis)
    return tuple((running[b:e].reshape(a.shape) for a, b, e in zip(arrays, ends, ends[1:])))


def derivative_jets(preact):
    gate_in = preact[:, 0]
    gate_dir = preact[:, 1]
    up_in = preact[:, 2]
    sigmoid_in = jax.nn.sigmoid(gate_in)
    first_slope = sigmoid_in * (1.0 + gate_in * (1.0 - sigmoid_in))
    second_slope = sigmoid_in * (1.0 - sigmoid_in) * (2.0 + gate_in * (1.0 - 2.0 * sigmoid_in))
    primal = gate_in * sigmoid_in * up_in
    tangent = first_slope * gate_dir * up_in
    second = second_slope * gate_dir * gate_dir * up_in
    return jnp.stack([primal, tangent, second], axis=1).astype(jnp.bfloat16)


def slot_numbers(flat_ids):
    number = jnp.arange(flat_ids.shape[0], dtype=jnp.int32)
    same = flat_ids[:, None] == flat_ids[None, :]
    return jnp.sum((same & (number[None, :] < number[:, None])).astype(jnp.int32), axis=1)


def slot_curvature(inv_root, moments, weighted_uu, resid_b, resid_a, resid_u):
    inv_cube = inv_root * inv_root * inv_root
    first_rate = 2.0 * moments[..., 0] / D
    second_rate = 2.0 * (moments[..., 1] + moments[..., 2]) / D
    slope_one = -0.5 * inv_cube * first_rate
    slope_two = (
        0.75 * inv_cube * inv_root * inv_root * first_rate * first_rate
        - 0.5 * inv_cube * second_rate
    )
    tangent_sq = (
        inv_root * inv_root * moments[..., 3]
        + 2.0 * inv_root * slope_one * moments[..., 4]
        + slope_one * slope_one * weighted_uu
    )
    bending = inv_root * resid_b + 2.0 * slope_one * resid_a + slope_two * resid_u
    return 2.0 * loss_weight / D * (tangent_sq + bending)


def on_device(tokens, targets, norm_gain, expert_ids, gate_prob, w_gate, gate_probe, w_up, w_down):
    tok_rows, width_part = tokens.shape
    hidden_part = w_gate.shape[1]
    holders = lax.axis_size("dp") // EXPERTS
    flat_ids = expert_ids.reshape(-1)
    places = flat_ids * CAP + slot_numbers(flat_ids)
    select = (places[:, None] == jnp.arange(EXPERTS * CAP, dtype=jnp.int32)).astype(jnp.bfloat16)
    outgoing = jnp.dot(
        jnp.sum(select.reshape(tok_rows, 2, -1), axis=1).astype(jnp.bfloat16).T,
        tokens,
        preferred_element_type=jnp.float32,
    ).astype(jnp.bfloat16)
    outgoing = jnp.repeat(outgoing.reshape(EXPERTS, CAP, width_part), holders, axis=0)
    arrived = lax.all_to_all(outgoing, "dp", split_axis=0, concat_axis=0, tiled=True)
    senders = arrived.shape[0]
    expert_rows = arrived.reshape(senders * CAP, width_part)
    partial_value = jnp.stack(
        [
            jnp.dot(expert_rows, w_gate, preferred_element_type=jnp.float32),
            jnp.dot(expert_rows, gate_probe, preferred_element_type=jnp.float32),
            jnp.dot(expert_rows, w_up, preferred_element_type=jnp.float32),
        ],
        axis=1,
    )
    hidden_jets = derivative_jets(
        of_everyone(partial_value.astype(jnp.bfloat16), "tensor").astype(jnp.float32)
    )
    images = jnp.dot(
        hidden_jets.reshape(-1, hidden_part), w_down, preferred_element_type=jnp.float32
    )
    images = images.reshape(senders, CAP, 3, width_part).astype(jnp.bfloat16)
    returned = lax.all_to_all(images, "dp", split_axis=0, concat_axis=0, tiled=True)
    grouped = jnp.sum(
        returned.astype(jnp.float32).reshape(EXPERTS, holders, CAP, 3, width_part), axis=1
    )
    grouped = grouped.astype(jnp.bfloat16).reshape(EXPERTS * CAP, 3 * width_part)
    chosen = jnp.dot(select, grouped, preferred_element_type=jnp.float32).astype(jnp.bfloat16)
    picked = of_everyone(chosen, "expert").reshape(tok_rows, 2, 3, width_part)
    weights = gate_prob[:, :, None]
    summed = tokens.astype(jnp.float32) + jnp.sum(weights * picked[:, :, 0], axis=1)
    tangent_out = weights * picked[:, :, 1]
    second_out = weights * picked[:, :, 2]
    target = targets.astype(jnp.float32)
    gain_sq = norm_gain * norm_gain
    spread_sum = summed[:, None, :]
    cross_ua = jnp.sum(spread_sum * tangent_out, axis=-1)
    along_aa = jnp.sum(tangent_out * tangent_out, axis=-1)
    cross_ub = jnp.sum(spread_sum * second_out, axis=-1)
    weighted_aa = jnp.sum(gain_sq * tangent_out * tangent_out, axis=-1)
    weighted_au = jnp.sum(gain_sq * spread_sum * tangent_out, axis=-1)
    gain_target = norm_gain * target
    weighted_ub = jnp.sum(gain_sq * spread_sum * second_out, axis=-1)
    target_b = jnp.sum(gain_target[:, None, :] * second_out, axis=-1)
    target_a = jnp.sum(gain_target[:, None, :] * tangent_out, axis=-1)
    token_stats = jnp.stack(
        [
            jnp.sum(summed * summed, axis=-1),
            jnp.sum(gain_sq * summed * summed, axis=-1),
            jnp.sum(gain_target * summed, axis=-1),
        ],
        axis=-1,
    )
    slot_stats = jnp.stack(
        [cross_ua, along_aa, cross_ub, weighted_aa, weighted_au, weighted_ub, target_b, target_a],
        axis=-1,
    )
    slot_total, token_total = packed_total((slot_stats, token_stats), "tensor")
    inv_root = lax.rsqrt(token_total[:, 0] / D + epsilon)[:, None]
    weighted_uu = token_total[:, 1:2]
    resid_b = inv_root * slot_total[..., 5] - slot_total[..., 6]
    resid_a = inv_root * slot_total[..., 4] - slot_total[..., 7]
    resid_u = inv_root * weighted_uu - token_total[:, 2:3]
    scaled = norm_gain * summed * inv_root
    normed = scaled.astype(jnp.bfloat16)
    curvature = slot_curvature(
        inv_root, slot_total[..., :5], weighted_uu, resid_b, resid_a, resid_u
    )
    member = (expert_ids[:, :, None] == jnp.arange(EXPERTS, dtype=jnp.int32)).astype(jnp.float32)
    totals, counts = packed_total(
        (jnp.sum(member * curvature[:, :, None], axis=(0, 1)), jnp.sum(member, axis=(0, 1))), "dp"
    )
    return (normed, curvature, totals / counts)


def solution(mesh):
    return jax.shard_map(
        on_device,
        mesh=mesh,
        in_specs=(
            P("dp", "tensor"),
            P("dp", "tensor"),
            P("tensor"),
            P("dp", None),
            P("dp", None),
            P("tensor", ("dp", "expert")),
            P("tensor", ("dp", "expert")),
            P("tensor", ("dp", "expert")),
            P(("dp", "expert"), "tensor"),
        ),
        out_specs=(P("dp", "tensor"), P("dp", None), P()),
        check_vma=False,
    )
```

```python
import functools

import jax
import jax.numpy as jnp
from jax import lax
from jax.experimental import pallas as pl
from jax.experimental.pallas import tpu as pltpu
from jax.sharding import PartitionSpec as P

D = 4096
EXPERTS = 8
TOK = 64
CAP = 18
MAIN = 16
FOLD = 8
PLANES = 4
OWNERS = 8
ROWS = OWNERS * CAP
WIDTH = 2048
PIECE = WIDTH // FOLD
BLOCK = WIDTH + PIECE
HIDDEN = 1024
HALF = HIDDEN // 2

epsilon = 1e-05
loss_weight = 8.0
bf16 = jnp.bfloat16
f32 = jnp.float32


def iota(shape, dim):
    return lax.broadcasted_iota(jnp.int32, shape, dim)


def ones_where(mask):
    return jnp.where(mask, 1.0, 0.0).astype(f32)


def dot(a, b):
    return jnp.dot(a, b, preferred_element_type=f32)


def slot_curvature(inv_root, moments, weighted_uu, resid_b, resid_a, resid_u):
    inv_cube = inv_root * inv_root * inv_root
    first_rate = 2.0 * moments[0] / D
    second_rate = 2.0 * (moments[1] + moments[2]) / D
    slope_one = -0.5 * inv_cube * first_rate
    slope_two = (
        0.75 * inv_cube * inv_root * inv_root * first_rate * first_rate
        - 0.5 * inv_cube * second_rate
    )
    tangent_sq = (
        inv_root * inv_root * moments[3]
        + 2.0 * inv_root * slope_one * moments[4]
        + slope_one * slope_one * weighted_uu
    )
    bending = inv_root * resid_b + 2.0 * slope_one * resid_a + slope_two * resid_u
    return 2.0 * loss_weight / D * (tangent_sq + bending)


def kernel(
    ids_ref, ids_row_ref, prob_ref, gain_ref, tokens_ref, targets_ref, wg_hbm, wp_hbm, wu_hbm, wd_hbm,
    normed_ref, curv_ref, est_ref,
    w_in, w_down, out_rows, rows, lhs, tsend, trecv, jets, folded, img, sib, ret,
    pown, prec, aown, asend, arec, bown, usum, stat, est_core, est_all,
    w_sem, d_send, d_recv, f_send, f_recv, t_send, t_recv, s_send, s_recv, r_send, r_recv,
    e_send, e_recv, st_send, st_recv, c_send, c_recv, a_send, a_recv,
):
    dp = lax.axis_index("dp")
    x_half = lax.axis_index("expert")
    part = lax.axis_index("tensor")
    z, y, core = dp // 8, (dp // 2) % 4, dp % 2
    chip = dp // 2
    sibling = {"dp": chip * 2 + (1 - core)}
    beside = {"tensor": 1 - part}
    across = {"expert": 1 - x_half}
    diagonal = {"expert": 1 - x_half, "tensor": 1 - part}

    def at(chip_index):
        return {"dp": chip_index * 2 + core}

    barrier = pltpu.get_barrier_semaphore()
    for who in (sibling, beside, across, diagonal):
        pl.semaphore_signal(barrier, inc=1, device_id=who)

    def greet(delta, _):
        pl.semaphore_signal(barrier, inc=1, device_id=at((chip + delta) % 16))
        return 0

    lax.fori_loop(1, 16, greet, 0)

    def weights(i):
        src = (wg_hbm, wp_hbm, wu_hbm)[i % 3].at[:, pl.ds((i // 3) * HALF, HALF)]
        return pltpu.make_async_copy(src, w_in.at[i], w_sem.at[i])

    for i in range(6):
        weights(i).start()
    down = pltpu.make_async_copy(wd_hbm, w_down, w_sem.at[6])
    down.start()

    ids = ids_ref[...]
    names = (ids[0:1, :] == iota((EXPERTS, TOK), 0)) | (ids[1:2, :] == iota((EXPERTS, TOK), 0))
    names = ones_where(names).astype(bf16)
    before = ones_where(iota((TOK, 2 * TOK), 0) < (iota((TOK, 2 * TOK), 1) & (TOK - 1))).astype(bf16)
    count = dot(names, before).astype(bf16)
    spread = ones_where((iota((128, EXPERTS), 0) >> 4) == iota((128, EXPERTS), 1)).astype(bf16)
    slot_of = dot(spread, count)[:, :TOK].astype(jnp.int32)
    named = dot(spread, names) > 0.5
    line = iota((128, TOK), 0)
    pick_main = ones_where(named & (slot_of == (line & 15))).astype(bf16)
    pick_fold = named & (slot_of == MAIN + (line & 1))
    out_rows[:, :, :WIDTH] = dot(pick_main, tokens_ref[...]).astype(bf16).reshape(EXPERTS, MAIN, WIDTH)
    fold = jnp.zeros((128, PIECE), f32)
    for f in range(FOLD):
        pick = ones_where(pick_fold & (((line >> 1) & 7) == f)).astype(bf16)
        fold = fold + dot(pick, tokens_ref[:, f * PIECE : (f + 1) * PIECE])
    out_rows[:, :, WIDTH:] = fold.astype(bf16).reshape(EXPERTS, MAIN, PIECE)

    pl.semaphore_wait(barrier, 19)

    def plane_of(j):
        return (z + (j + y) % PLANES) % PLANES

    def dispatch(j, q):
        target = plane_of(j) * 4 + q
        block = out_rows.at[plane_of(j) * 2 + q // 2]
        here = pltpu.make_async_copy(block, rows.at[j, core, y], d_recv.at[j, y])
        there = pltpu.make_async_remote_copy(
            src_ref=block, dst_ref=rows.at[j, core, y], send_sem=d_send.at[j, q], recv_sem=d_recv.at[j, y],
            device_id=at(target),
        )
        return target == chip, here, there

    def start_dispatch(j):
        def one(q, _):
            mine, here, there = dispatch(j, q)

            @pl.when(mine)
            def _():
                here.start()

            @pl.when(jnp.logical_not(mine))
            def _():
                there.start()

            return 0

        lax.fori_loop(0, 4, one, 0)

    def end_dispatch(j):
        def one(q, _):
            mine, _, there = dispatch(j, q)

            @pl.when(jnp.logical_not(mine))
            def _():
                there.wait_send()

            return 0

        lax.fori_loop(0, 4, one, 0)

    def passed_on(j):
        return pltpu.make_async_remote_copy(
            src_ref=rows.at[j, core], dst_ref=rows.at[j, core], send_sem=f_send.at[j], recv_sem=f_recv.at[j],
            device_id=sibling,
        )

    def arrive(j):
        def one(q, _):
            pltpu.make_async_copy(out_rows.at[0], rows.at[j, core, q], d_recv.at[j, q]).wait()
            return 0

        lax.fori_loop(0, 4, one, 0)
        passed_on(j).start()

    a_, b_ = iota((128, 128), 0), iota((128, 128), 1)
    swap = ones_where(
        ((a_ >> 4) == ((b_ >> 1) & 7)) & (((a_ >> 1) & 7) == (b_ >> 4)) & ((a_ & 1) == (b_ & 1))
    ).astype(bf16)

    def exchange(j, i):
        return pltpu.make_async_remote_copy(
            src_ref=tsend.at[j, i], dst_ref=trecv.at[j, i], send_sem=t_send.at[j, i], recv_sem=t_recv.at[j, i],
            device_id=beside,
        )

    def project(j, send):
        passed_on(j).wait_recv()
        lhs[: OWNERS * MAIN, :] = rows[j, :, :, :, :WIDTH].reshape(OWNERS * MAIN, WIDTH)
        extra = rows[j, :, :, :, WIDTH:].reshape(128, PIECE)
        extra = dot(swap, extra).astype(bf16)
        for f in range(FOLD):
            lhs[OWNERS * MAIN :, f * PIECE : (f + 1) * PIECE] = extra[f * 16 : (f + 1) * 16]

        def one(i, _):
            if j == 0:
                pltpu.make_async_copy(w_in.at[i], w_in.at[i], w_sem.at[i]).wait()
            tsend[j, i] = dot(lhs[...], w_in[i]).astype(bf16)
            if send:
                exchange(j, i).start()
            return 0

        lax.fori_loop(0, 6, one, 0)

    def to_sibling(j):
        return pltpu.make_async_remote_copy(
            src_ref=img.at[j, 1 - core], dst_ref=sib.at[j], send_sem=s_send.at[j], recv_sem=s_recv.at[j],
            device_id=sibling,
        )

    def expand(j):
        for half in range(2):
            for i in range(3):
                exchange(j, half * 3 + i).wait_recv()
            if j < PLANES - 1:
                for i in range(3):
                    exchange(j + 1, half * 3 + i).start()

            def one(block, _):
                at_ = pl.ds(pl.multiple_of(block * 16, 16), 16)

                def pre(i):
                    return tsend[j, half * 3 + i, at_].astype(f32) + trecv[j, half * 3 + i, at_].astype(f32)

                g, d, u = pre(0), pre(1), pre(2)
                s = jax.nn.sigmoid(g)
                first = s * (1.0 + g * (1.0 - s))
                second = s * (1.0 - s) * (2.0 + g * (1.0 - 2.0 * s))
                cols = slice(half * HALF, (half + 1) * HALF)
                jets[at_, cols] = (g * s * u).astype(bf16)
                jets[pl.ds(pl.multiple_of(ROWS + block * 16, 16), 16), cols] = (first * d * u).astype(bf16)
                jets[pl.ds(pl.multiple_of(2 * ROWS + block * 16, 16), 16), cols] = (second * d * d * u).astype(bf16)
                return 0

            lax.fori_loop(0, ROWS // 16, one, 0)
        if j == 0:
            down.wait()

        def piece(n, _):
            cols = pl.ds(pl.multiple_of(n * PIECE, PIECE), PIECE)
            out = dot(jets[...], w_down[:, cols]).astype(bf16)
            for i in range(3):
                top = i * ROWS
                img[j, :, :, i, :, cols] = out[top : top + 128].reshape(2, 4, MAIN, PIECE)
                folded[i, pl.ds(pl.multiple_of(n * 16, 16), 16)] = out[top + 128 : top + 144]
            return 0

        lax.fori_loop(0, FOLD, piece, 0)
        for i in range(3):
            extra = dot(swap, folded[i]).astype(bf16)
            img[j, :, :, i, :, WIDTH:] = extra.reshape(2, 4, MAIN, PIECE)
        to_sibling(j).start()

    def give(j, q):
        target = ((z + PLANES - (j + q) % PLANES) % PLANES) * 4 + q
        here = pltpu.make_async_copy(img.at[j, core, q], ret.at[j, y], r_recv.at[j, y])
        there = pltpu.make_async_remote_copy(
            src_ref=img.at[j, core, q], dst_ref=ret.at[j, y], send_sem=r_send.at[j, q], recv_sem=r_recv.at[j, y],
            device_id=at(target),
        )
        return target == chip, here, there

    def give_back(j):
        to_sibling(j).wait_recv()

        def one(q, _):
            img[j, core, q] = (img[j, core, q].astype(f32) + sib[j, q].astype(f32)).astype(bf16)
            mine, here, there = give(j, q)

            @pl.when(mine)
            def _():
                here.start()

            @pl.when(jnp.logical_not(mine))
            def _():
                there.start()

            return 0

        lax.fori_loop(0, 4, one, 0)

    start_dispatch(0)
    arrive(0)
    for j in range(1, PLANES):
        start_dispatch(j)
    project(0, True)
    arrive(1)
    project(1, False)
    arrive(2)
    arrive(3)
    expand(0)
    project(2, False)
    give_back(0)
    expand(1)
    project(3, False)
    give_back(1)
    expand(2)
    give_back(2)
    expand(3)

    ids_row = ids_row_ref[...]
    line = iota((256, 2 * TOK), 0)
    plane = (z + (((line >> 6) + y) & 3)) & 3
    expert_of = plane * 2 + ((line >> 5) & 1)
    small = iota((256, EXPERTS), 0)
    small = ((z + (((small >> 6) + y) & 3)) & 3) * 2 + ((small >> 5) & 1)
    spread_back = ones_where(small == iota((256, EXPERTS), 1)).astype(bf16)
    slot_back = dot(spread_back, count).astype(jnp.int32)
    mine = expert_of == ids_row
    back_main = ones_where(mine & (slot_back == (line & 15))).T.astype(bf16)
    back_fold = ones_where(mine & (slot_back == MAIN + (line & 1))).T
    fold_index = (iota((2 * TOK, 256), 1) >> 1) & 7
    eye = a_ == b_
    prob_col = jnp.sum(jnp.where(eye, prob_ref[...], 0.0), axis=1, keepdims=True)
    id_col = jnp.sum(jnp.where(eye, ids_row.astype(f32), 0.0), axis=1, keepdims=True)

    give_back(3)
    for j in range(PLANES):
        for q in range(4):
            pltpu.make_async_copy(ret.at[j, q], ret.at[j, q], r_recv.at[j, q]).wait()

    def pieces(f, _):
        cols = pl.ds(pl.multiple_of(f * PIECE, PIECE), PIECE)
        pick = jnp.where(fold_index == f, back_fold, 0.0).astype(bf16)

        def picked(i):
            whole = ret[:, :, i, :, cols].reshape(256, PIECE)
            extra = ret[:, :, i, :, WIDTH:].reshape(256, PIECE)
            return prob_col * (dot(back_main, whole) + dot(pick, extra))

        value = picked(0)
        pown[:, cols] = (value[:TOK] + value[TOK:]).astype(bf16)
        half_cols = pl.ds(pl.multiple_of((f % 4) * PIECE, PIECE), PIECE)
        tangent = picked(1)
        aown[f // 4, :, half_cols] = tangent
        asend[f // 4, :, half_cols] = tangent.astype(bf16)
        bown[:, cols] = picked(2)
        return 0

    lax.fori_loop(0, FOLD, pieces, 0)
    value_copy = pltpu.make_async_remote_copy(
        src_ref=pown, dst_ref=prec, send_sem=e_send.at[0], recv_sem=e_recv.at[0], device_id=across
    )
    tangent_copy = pltpu.make_async_remote_copy(
        src_ref=asend.at[1 - x_half], dst_ref=arec, send_sem=e_send.at[1], recv_sem=e_recv.at[1], device_id=across
    )
    value_copy.start()
    tangent_copy.start()
    value_copy.wait_recv()
    tangent_copy.wait_recv()

    me = x_half * 2 + part
    lane = iota((16, 128), 1)
    near = pl.ds(pl.multiple_of(x_half * (WIDTH // 2), WIDTH // 2), WIDTH // 2)

    def inner(block, _):
        at_ = pl.ds(pl.multiple_of(block * 16, 16), 16)
        u = tokens_ref[at_].astype(f32) + (pown[at_].astype(f32) + prec[at_].astype(f32))
        usum[at_] = u
        gain = gain_ref[...]
        heavy = gain * gain * u
        goal = gain * targets_ref[at_].astype(f32)
        stats = [None] * 19

        def over(v):
            return jnp.sum(v, axis=-1, keepdims=True)

        for k in range(2):
            b = bown[pl.ds(pl.multiple_of(k * TOK + block * 16, 16), 16)]
            stats[3 + k * 8 + 2] = over(u * b)
            stats[3 + k * 8 + 5] = over(heavy * b)
            stats[3 + k * 8 + 6] = over(goal * b)
        gain = gain_ref[:, near]
        u = usum[at_, near]
        heavy = gain * gain * u
        goal = gain * targets_ref[at_, near].astype(f32)
        stats[0] = over(u * u)
        stats[1] = over(heavy * u)
        stats[2] = over(goal * u)
        for k in range(2):
            own = pl.ds(pl.multiple_of(k * TOK + block * 16, 16), 16)
            a = aown[x_half, own] + arec[own].astype(f32)
            stats[3 + k * 8 + 0] = over(u * a)
            stats[3 + k * 8 + 1] = over(a * a)
            stats[3 + k * 8 + 3] = over(gain * gain * a * a)
            stats[3 + k * 8 + 4] = over(heavy * a)
            stats[3 + k * 8 + 7] = over(goal * a)
        laid = jnp.zeros((16, 128), f32)
        for i, value in enumerate(stats):
            laid = jnp.where(lane == i, value, laid)
        stat[me, at_] = laid
        return 0

    lax.fori_loop(0, TOK // 16, inner, 0)

    def stat_copy(i, who):
        return pltpu.make_async_remote_copy(
            src_ref=stat.at[me], dst_ref=stat.at[me], send_sem=st_send.at[i], recv_sem=st_recv.at[i], device_id=who
        )

    for i, who in enumerate((beside, across, diagonal)):
        stat_copy(i, who).start()
    for i, who in enumerate((beside, across, diagonal)):
        stat_copy(i, who).wait_recv()
    total = (stat[0] + stat[1]) + (stat[2] + stat[3])

    def column(i):
        return total[:, i : i + 1]

    inv_root = lax.rsqrt(column(0) / D + epsilon)
    weighted_uu = column(1)
    resid_u = inv_root * weighted_uu - column(2)
    sums = jnp.zeros((1, 128), f32)
    pairs = jnp.zeros((1, 128), f32)
    eye_tok = iota((TOK, TOK), 0) == iota((TOK, TOK), 1)
    for k in range(2):
        m = [column(3 + k * 8 + i) for i in range(8)]
        curve = slot_curvature(
            inv_root, m[:5], weighted_uu, inv_root * m[5] - m[6], inv_root * m[4] - m[7], resid_u
        )
        curv_ref[k : k + 1, :] = jnp.sum(jnp.where(eye_tok, curve, 0.0), axis=0, keepdims=True)
        member = ones_where(iota((TOK, 128), 1).astype(f32) == id_col[k * TOK : (k + 1) * TOK])
        sums = sums + jnp.sum(member * curve, axis=0, keepdims=True)
        pairs = pairs + jnp.sum(member, axis=0, keepdims=True)
    row = iota((8, 128), 0)
    est_core[core] = jnp.where(row == 0, sums, jnp.where(row == 1, pairs, 0.0))
    core_copy = pltpu.make_async_remote_copy(
        src_ref=est_core.at[core], dst_ref=est_core.at[core], send_sem=c_send, recv_sem=c_recv, device_id=sibling
    )
    core_copy.start()
    core_copy.wait_recv()
    est_all[chip] = est_core[0] + est_core[1]

    def all_copy(delta):
        return pltpu.make_async_remote_copy(
            src_ref=est_all.at[chip], dst_ref=est_all.at[chip], send_sem=a_send.at[delta], recv_sem=a_recv.at[delta],
            device_id=at((chip + delta) % 16),
        )

    def start_all(delta, _):
        all_copy(delta).start()
        return 0

    lax.fori_loop(1, 16, start_all, 0)
    for block in range(TOK // 16):
        at_ = slice(block * 16, (block + 1) * 16)
        normed_ref[at_] = (gain_ref[...] * usum[at_] * inv_root[at_]).astype(bf16)

    for j in range(PLANES):
        end_dispatch(j)
        passed_on(j).wait_send()
        for i in range(6):
            exchange(j, i).wait_send()
        to_sibling(j).wait_send()

        def gone(q, _):
            mine, _, there = give(j, q)

            @pl.when(jnp.logical_not(mine))
            def _():
                there.wait_send()

            return 0

        lax.fori_loop(0, 4, gone, 0)
    value_copy.wait_send()
    tangent_copy.wait_send()
    for i, who in enumerate((beside, across, diagonal)):
        stat_copy(i, who).wait_send()
    core_copy.wait_send()

    def end_all(delta, _):
        all_copy(delta).wait()
        return 0

    lax.fori_loop(1, 16, end_all, 0)
    final = jnp.sum(est_all[...], axis=0)
    est_ref[...] = final[0:1] / jnp.maximum(final[1:2], 1.0)


def on_device(tokens, targets, norm_gain, expert_ids, gate_prob, w_gate, gate_probe, w_up, w_down):
    vmem = pl.BlockSpec(memory_space=pltpu.VMEM)
    anywhere = pl.BlockSpec(memory_space=pl.ANY)
    dma = pltpu.SemaphoreType.DMA
    normed, curvature, estimate = pl.pallas_call(
        kernel,
        out_shape=(
            jax.ShapeDtypeStruct((TOK, WIDTH), bf16),
            jax.ShapeDtypeStruct((2, TOK), f32),
            jax.ShapeDtypeStruct((1, 128), f32),
        ),
        in_specs=[vmem] * 6 + [anywhere] * 4,
        out_specs=(vmem, vmem, vmem),
        scratch_shapes=[
            pltpu.VMEM((6, WIDTH, HALF), bf16),
            pltpu.VMEM((HIDDEN, WIDTH), bf16),
            pltpu.VMEM((EXPERTS, MAIN, BLOCK), bf16),
            pltpu.VMEM((PLANES, 2, 4, MAIN, BLOCK), bf16),
            pltpu.VMEM((ROWS, WIDTH), bf16),
            pltpu.VMEM((PLANES, 6, ROWS, HALF), bf16),
            pltpu.VMEM((PLANES, 6, ROWS, HALF), bf16),
            pltpu.VMEM((3 * ROWS, HIDDEN), bf16),
            pltpu.VMEM((3, 128, PIECE), bf16),
            pltpu.VMEM((PLANES, 2, 4, 3, MAIN, BLOCK), bf16),
            pltpu.VMEM((PLANES, 4, 3, MAIN, BLOCK), bf16),
            pltpu.VMEM((PLANES, 4, 3, MAIN, BLOCK), bf16),
            pltpu.VMEM((TOK, WIDTH), bf16),
            pltpu.VMEM((TOK, WIDTH), bf16),
            pltpu.VMEM((2, 2 * TOK, WIDTH // 2), f32),
            pltpu.VMEM((2, 2 * TOK, WIDTH // 2), bf16),
            pltpu.VMEM((2 * TOK, WIDTH // 2), bf16),
            pltpu.VMEM((2 * TOK, WIDTH), f32),
            pltpu.VMEM((TOK, WIDTH), f32),
            pltpu.VMEM((4, TOK, 128), f32),
            pltpu.VMEM((2, 8, 128), f32),
            pltpu.VMEM((16, 8, 128), f32),
            dma((7,)),
            dma((PLANES, 4)), dma((PLANES, 4)),
            dma((PLANES,)), dma((PLANES,)),
            dma((PLANES, 6)), dma((PLANES, 6)),
            dma((PLANES,)), dma((PLANES,)),
            dma((PLANES, 4)), dma((PLANES, 4)),
            dma((2,)), dma((2,)),
            dma((3,)), dma((3,)),
            dma, dma,
            dma((16,)), dma((16,)),
        ],
        compiler_params=pltpu.CompilerParams(
            collective_id=0, has_side_effects=True, vmem_limit_bytes=60 * 1024 * 1024
        ),
    )(
        expert_ids.T,
        expert_ids.T.reshape(1, 2 * TOK),
        gate_prob.T.reshape(1, 2 * TOK),
        norm_gain.reshape(1, WIDTH),
        tokens,
        targets,
        w_gate,
        gate_probe,
        w_up,
        w_down,
    )
    return normed, curvature.T, estimate[0, :EXPERTS]


def solution(mesh):
    return jax.shard_map(
        on_device,
        mesh=mesh,
        in_specs=(
            P("dp", "tensor"),
            P("dp", "tensor"),
            P("tensor"),
            P("dp", None),
            P("dp", None),
            P("tensor", ("dp", "expert")),
            P("tensor", ("dp", "expert")),
            P("tensor", ("dp", "expert")),
            P(("dp", "expert"), "tensor"),
        ),
        out_specs=(P("dp", "tensor"), P("dp", None), P()),
        check_vma=False,
    )
```

```python
import functools

import jax
import jax.numpy as jnp
from jax import lax
from jax.experimental import pallas as pl
from jax.experimental.pallas import tpu as pltpu
from jax.sharding import PartitionSpec as P

D = 4096
EXPERTS = 8
TOK = 64
CAP = 18
MAIN = 16
FOLD = 8
PLANES = 4
OWNERS = 8
ROWS = OWNERS * CAP
WIDTH = 2048
PIECE = WIDTH // FOLD
BLOCK = WIDTH + PIECE
HIDDEN = 1024
HALF = HIDDEN // 2
OWN = (0, 64)
OTHER = (64, 80)

epsilon = 1e-05
loss_weight = 8.0
bf16 = jnp.bfloat16
f32 = jnp.float32


def iota(shape, dim):
    return lax.broadcasted_iota(jnp.int32, shape, dim)


def ones_where(mask):
    return jnp.where(mask, 1.0, 0.0).astype(f32)


def dot(a, b):
    return jnp.dot(a, b, preferred_element_type=f32)


def slot_curvature(inv_root, moments, weighted_uu, resid_b, resid_a, resid_u):
    inv_cube = inv_root * inv_root * inv_root
    first_rate = 2.0 * moments[0] / D
    second_rate = 2.0 * (moments[1] + moments[2]) / D
    slope_one = -0.5 * inv_cube * first_rate
    slope_two = (
        0.75 * inv_cube * inv_root * inv_root * first_rate * first_rate
        - 0.5 * inv_cube * second_rate
    )
    tangent_sq = (
        inv_root * inv_root * moments[3]
        + 2.0 * inv_root * slope_one * moments[4]
        + slope_one * slope_one * weighted_uu
    )
    bending = inv_root * resid_b + 2.0 * slope_one * resid_a + slope_two * resid_u
    return 2.0 * loss_weight / D * (tangent_sq + bending)


def kernel(
    ids_ref, prob_ref, gain_ref, tokens_ref, targets_ref, wg_hbm, wp_hbm, wu_hbm, wd_hbm,
    normed_ref, small_ref,
    w_in, w_down, out_rows, rows, lhs, tsend, trecv, jets, folded, img, sib, ret,
    pown, prec, aown, asend, arec, bown, usum, stat, est_core, est_all,
    w_sem, d_send, d_recv, f_send, f_recv, t_send, t_recv, s_send, s_recv, r_send, r_recv,
    e_send, e_recv, st_send, st_recv, c_send, c_recv, a_send, a_recv,
):
    dp = lax.axis_index("dp")
    x_half = lax.axis_index("expert")
    part = lax.axis_index("tensor")
    z, y, core = dp // 8, (dp // 2) % 4, dp % 2
    chip = dp // 2
    sibling = {"dp": chip * 2 + (1 - core)}
    beside = {"tensor": 1 - part}
    across = {"expert": 1 - x_half}
    diagonal = {"expert": 1 - x_half, "tensor": 1 - part}

    def at(chip_index):
        return {"dp": chip_index * 2 + core}

    barrier = pltpu.get_barrier_semaphore()
    for who in (sibling, beside, across, diagonal):
        pl.semaphore_signal(barrier, inc=1, device_id=who)

    def greet(delta, _):
        pl.semaphore_signal(barrier, inc=1, device_id=at((chip + delta) % 16))
        return 0

    lax.fori_loop(1, 16, greet, 0)

    def weights(i):
        src = (wg_hbm, wp_hbm, wu_hbm)[i // 2].at[:, pl.ds((i % 2) * HALF, HALF)]
        return pltpu.make_async_copy(src, w_in.at[i], w_sem.at[i])

    for i in range(6):
        weights(i).start()
    down = pltpu.make_async_copy(wd_hbm, w_down, w_sem.at[6])
    down.start()

    ids = ids_ref[...]
    names = (ids[0:1, :] == iota((EXPERTS, TOK), 0)) | (ids[1:2, :] == iota((EXPERTS, TOK), 0))
    names = ones_where(names).astype(bf16)
    before = ones_where(iota((TOK, TOK), 0) < iota((TOK, TOK), 1)).astype(bf16)
    count = dot(names, before).astype(bf16)
    spread = ones_where((iota((128, EXPERTS), 0) >> 4) == iota((128, EXPERTS), 1)).astype(bf16)
    slot_of = dot(spread, count).astype(jnp.int32)
    named = dot(spread, names) > 0.5
    line = iota((128, TOK), 0)
    pick_main = ones_where(named & (slot_of == (line & 15))).astype(bf16)
    pick_fold = named & (slot_of == MAIN + (line & 1))
    out_rows[:, :, :WIDTH] = dot(pick_main, tokens_ref[...]).astype(bf16).reshape(EXPERTS, MAIN, WIDTH)
    fold = jnp.zeros((128, PIECE), f32)
    for f in range(FOLD):
        pick = ones_where(pick_fold & (((line >> 1) & 7) == f)).astype(bf16)
        fold = fold + dot(pick, tokens_ref[:, f * PIECE : (f + 1) * PIECE])
    out_rows[:, :, WIDTH:] = fold.astype(bf16).reshape(EXPERTS, MAIN, PIECE)

    pl.semaphore_wait(barrier, 19)

    def plane_of(j):
        return (z + (j + y) % PLANES) % PLANES

    def dispatch(j, q):
        target = plane_of(j) * 4 + q
        block = out_rows.at[plane_of(j) * 2 + q // 2]
        here = pltpu.make_async_copy(block, rows.at[j, core, y], d_recv.at[j, y])
        there = pltpu.make_async_remote_copy(
            src_ref=block, dst_ref=rows.at[j, core, y], send_sem=d_send.at[j, q], recv_sem=d_recv.at[j, y],
            device_id=at(target),
        )
        return target == chip, here, there

    def start_dispatch(j):
        def one(q, _):
            mine, here, there = dispatch(j, q)

            @pl.when(mine)
            def _():
                here.start()

            @pl.when(jnp.logical_not(mine))
            def _():
                there.start()

            return 0

        lax.fori_loop(0, 4, one, 0)

    def end_dispatch(j):
        def one(q, _):
            mine, _, there = dispatch(j, q)

            @pl.when(jnp.logical_not(mine))
            def _():
                there.wait_send()

            return 0

        lax.fori_loop(0, 4, one, 0)

    def passed_on(j):
        return pltpu.make_async_remote_copy(
            src_ref=rows.at[j, core], dst_ref=rows.at[j, core], send_sem=f_send.at[j], recv_sem=f_recv.at[j],
            device_id=sibling,
        )

    def arrive(j):
        def one(q, _):
            pltpu.make_async_copy(out_rows.at[0], rows.at[j, core, q], d_recv.at[j, q]).wait()
            return 0

        lax.fori_loop(0, 4, one, 0)
        passed_on(j).start()

    a_, b_ = iota((128, 128), 0), iota((128, 128), 1)
    swap = ones_where(
        ((a_ >> 4) == ((b_ >> 1) & 7)) & (((a_ >> 1) & 7) == (b_ >> 4)) & ((a_ & 1) == (b_ & 1))
    ).astype(bf16)

    def exchange(j, unit, i):
        at_ = pl.ds(*unit)
        number = 0 if unit == OWN else 1
        return pltpu.make_async_remote_copy(
            src_ref=tsend.at[j, i, at_], dst_ref=trecv.at[j, i, at_],
            send_sem=t_send.at[j, number, i], recv_sem=t_recv.at[j, number, i], device_id=beside,
        )

    def project(j, unit, send):
        first, many = unit
        at_ = slice(first, first + many)
        if unit == OWN:
            lhs[at_, :] = rows[j, core, :, :, :WIDTH].reshape(64, WIDTH)
        else:
            passed_on(j).wait_recv()
            lhs[64:128, :] = rows[j, 1 - core, :, :, :WIDTH].reshape(64, WIDTH)
            extra = rows[j, :, :, :, WIDTH:].reshape(128, PIECE)
            extra = dot(swap, extra).astype(bf16)
            for f in range(FOLD):
                lhs[128:, f * PIECE : (f + 1) * PIECE] = extra[f * 16 : (f + 1) * 16]

        def one(i, _):
            for half in range(2):
                w = i * 2 + half
                if j == 0 and unit == OWN:
                    pltpu.make_async_copy(w_in.at[w], w_in.at[w], w_sem.at[w]).wait()
                tsend[j, i, at_, half * HALF : (half + 1) * HALF] = dot(lhs[at_, :], w_in[w]).astype(bf16)
            if send:
                exchange(j, unit, i).start()
            return 0

        lax.fori_loop(0, 3, one, 0)

    def to_sibling(j):
        return pltpu.make_async_remote_copy(
            src_ref=img.at[j, 1 - core], dst_ref=sib.at[j], send_sem=s_send.at[j], recv_sem=s_recv.at[j],
            device_id=sibling,
        )

    def expand(j, unit, following):
        first, many = unit
        for i in range(3):
            exchange(j, unit, i).wait_recv()
        if following:
            for i in range(3):
                exchange(*following, i).start()

        def one(block, _):
            at_ = pl.ds(pl.multiple_of(first + block * 16, 16), 16)

            def pre(i):
                return tsend[j, i, at_].astype(f32) + trecv[j, i, at_].astype(f32)

            g, d, u = pre(0), pre(1), pre(2)
            s = jax.nn.sigmoid(g)
            slope = s * (1.0 + g * (1.0 - s))
            second = s * (1.0 - s) * (2.0 + g * (1.0 - 2.0 * s))
            jets[pl.ds(pl.multiple_of(block * 16, 16), 16)] = (g * s * u).astype(bf16)
            jets[pl.ds(pl.multiple_of(many + block * 16, 16), 16)] = (slope * d * u).astype(bf16)
            jets[pl.ds(pl.multiple_of(2 * many + block * 16, 16), 16)] = (second * d * d * u).astype(bf16)
            return 0

        lax.fori_loop(0, many // 16, one, 0)
        if j == 0 and unit == OWN:
            down.wait()
        whose = core if unit == OWN else 1 - core

        def piece(n, _):
            cols = pl.ds(pl.multiple_of(n * PIECE, PIECE), PIECE)
            out = dot(jets[: 3 * many], w_down[:, cols]).astype(bf16)
            for i in range(3):
                top = i * many
                img[j, whose, :, i, :, cols] = out[top : top + 64].reshape(4, MAIN, PIECE)
                if unit != OWN:
                    folded[i, pl.ds(pl.multiple_of(n * 16, 16), 16)] = out[top + 64 : top + 80]
            return 0

        lax.fori_loop(0, FOLD, piece, 0)
        if unit != OWN:
            for i in range(3):
                extra = dot(swap, folded[i]).astype(bf16)
                img[j, :, :, i, :, WIDTH:] = extra.reshape(2, 4, MAIN, PIECE)
            to_sibling(j).start()

    def give(j, q):
        target = ((z + PLANES - (j + q) % PLANES) % PLANES) * 4 + q
        here = pltpu.make_async_copy(img.at[j, core, q], ret.at[j, y], r_recv.at[j, y])
        there = pltpu.make_async_remote_copy(
            src_ref=img.at[j, core, q], dst_ref=ret.at[j, y], send_sem=r_send.at[j, q], recv_sem=r_recv.at[j, y],
            device_id=at(target),
        )
        return target == chip, here, there

    def give_back(j):
        to_sibling(j).wait_recv()

        def one(q, _):
            img[j, core, q] = (img[j, core, q].astype(f32) + sib[j, q].astype(f32)).astype(bf16)
            mine, here, there = give(j, q)

            @pl.when(mine)
            def _():
                here.start()

            @pl.when(jnp.logical_not(mine))
            def _():
                there.start()

            return 0

        lax.fori_loop(0, 4, one, 0)

    units = [(0, OWN), (0, OTHER)] + [(j, unit) for j in range(1, PLANES) for unit in (OTHER, OWN)]
    start_dispatch(0)
    arrive(0)
    project(*units[0], True)
    for j in range(1, PLANES):
        start_dispatch(j)
    project(*units[1], True)
    arrive(1)
    project(*units[2], False)
    arrive(2)
    arrive(3)
    for n, (j, unit) in enumerate(units):
        expand(j, unit, units[n + 2] if n + 2 < len(units) else None)
        if n + 3 < len(units):
            project(*units[n + 3], False)
        if n == 2:
            give_back(0)
        if j > 0 and unit == OWN:
            give_back(j)

    line = iota((256, TOK), 0)
    plane = (z + (((line >> 6) + y) & 3)) & 3
    expert_of = plane * 2 + ((line >> 5) & 1)
    small = iota((256, EXPERTS), 0)
    small = ((z + (((small >> 6) + y) & 3)) & 3) * 2 + ((small >> 5) & 1)
    spread_back = ones_where(small == iota((256, EXPERTS), 1)).astype(bf16)
    slot_back = dot(spread_back, count).astype(jnp.int32)
    eye_tok = iota((TOK, TOK), 0) == iota((TOK, TOK), 1)

    def upright(row):
        return jnp.sum(jnp.where(eye_tok, row, 0.0), axis=1, keepdims=True)

    def for_ids(make):
        return jnp.concatenate([make(ids[k : k + 1, :]) for k in range(2)], axis=0)

    back_main = for_ids(lambda row: ones_where((expert_of == row) & (slot_back == (line & 15))).T).astype(bf16)
    back_fold = for_ids(lambda row: ones_where((expert_of == row) & (slot_back == MAIN + (line & 1))).T)
    fold_index = (iota((2 * TOK, 256), 1) >> 1) & 7
    prob_col = jnp.concatenate([upright(prob_ref[k : k + 1, :]) for k in range(2)], axis=0)
    id_col = [upright(ids[k : k + 1, :].astype(f32)) for k in range(2)]

    for j in range(PLANES):
        for q in range(4):
            pltpu.make_async_copy(ret.at[j, q], ret.at[j, q], r_recv.at[j, q]).wait()

    def picked(i, f):
        pick = jnp.where(fold_index == f, back_fold, 0.0).astype(bf16)
        whole = ret[:, :, i, :, pl.ds(pl.multiple_of(f * PIECE, PIECE), PIECE)].reshape(256, PIECE)
        extra = ret[:, :, i, :, WIDTH:].reshape(256, PIECE)
        return prob_col * (dot(back_main, whole) + dot(pick, extra))

    def values(f, _):
        value = picked(0, f)
        pown[:, pl.ds(pl.multiple_of(f * PIECE, PIECE), PIECE)] = (value[:TOK] + value[TOK:]).astype(bf16)
        return 0

    def tangents(f, _):
        half_cols = pl.ds(pl.multiple_of((f % 4) * PIECE, PIECE), PIECE)
        tangent = picked(1, f)
        aown[f // 4, :, half_cols] = tangent
        asend[f // 4, :, half_cols] = tangent.astype(bf16)
        return 0

    def seconds(f, _):
        bown[:, pl.ds(pl.multiple_of(f * PIECE, PIECE), PIECE)] = picked(2, f)
        return 0

    value_copy = pltpu.make_async_remote_copy(
        src_ref=pown, dst_ref=prec, send_sem=e_send.at[0], recv_sem=e_recv.at[0], device_id=across
    )
    tangent_copy = pltpu.make_async_remote_copy(
        src_ref=asend.at[1 - x_half], dst_ref=arec, send_sem=e_send.at[1], recv_sem=e_recv.at[1], device_id=across
    )
    lax.fori_loop(0, FOLD, values, 0)
    value_copy.start()
    lax.fori_loop(0, FOLD, tangents, 0)
    tangent_copy.start()
    lax.fori_loop(0, FOLD, seconds, 0)

    me = x_half * 2 + part
    lane = iota((16, 128), 1)
    near = pl.ds(pl.multiple_of(x_half * (WIDTH // 2), WIDTH // 2), WIDTH // 2)

    def over(v):
        return jnp.sum(v, axis=-1, keepdims=True)

    def lay(values, laid):
        for i, value in values.items():
            laid = jnp.where(lane == i, value, laid)
        return laid

    def inner_value(block, _):
        at_ = pl.ds(pl.multiple_of(block * 16, 16), 16)
        u = tokens_ref[at_].astype(f32) + (pown[at_].astype(f32) + prec[at_].astype(f32))
        usum[at_] = u
        gain = gain_ref[...]
        heavy = gain * gain * u
        goal = gain * targets_ref[at_].astype(f32)
        stats = {}
        for k in range(2):
            b = bown[pl.ds(pl.multiple_of(k * TOK + block * 16, 16), 16)]
            stats[3 + k * 8 + 2] = over(u * b)
            stats[3 + k * 8 + 5] = over(heavy * b)
            stats[3 + k * 8 + 6] = over(goal * b)
        gain = gain_ref[:, near]
        u = usum[at_, near]
        heavy = gain * gain * u
        goal = gain * targets_ref[at_, near].astype(f32)
        stats[0] = over(u * u)
        stats[1] = over(heavy * u)
        stats[2] = over(goal * u)
        stat[me, at_] = lay(stats, jnp.zeros((16, 128), f32))
        return 0

    def inner_tangent(block, _):
        at_ = pl.ds(pl.multiple_of(block * 16, 16), 16)
        gain = gain_ref[:, near]
        u = usum[at_, near]
        heavy = gain * gain * u
        goal = gain * targets_ref[at_, near].astype(f32)
        stats = {}
        for k in range(2):
            own = pl.ds(pl.multiple_of(k * TOK + block * 16, 16), 16)
            a = aown[x_half, own] + arec[own].astype(f32)
            stats[3 + k * 8 + 0] = over(u * a)
            stats[3 + k * 8 + 1] = over(a * a)
            stats[3 + k * 8 + 3] = over(gain * gain * a * a)
            stats[3 + k * 8 + 4] = over(heavy * a)
            stats[3 + k * 8 + 7] = over(goal * a)
        stat[me, at_] = lay(stats, stat[me, at_])
        return 0

    value_copy.wait_recv()
    lax.fori_loop(0, TOK // 16, inner_value, 0)
    tangent_copy.wait_recv()
    lax.fori_loop(0, TOK // 16, inner_tangent, 0)

    def stat_copy(i, who):
        return pltpu.make_async_remote_copy(
            src_ref=stat.at[me], dst_ref=stat.at[me], send_sem=st_send.at[i], recv_sem=st_recv.at[i], device_id=who
        )

    for i, who in enumerate((beside, across, diagonal)):
        stat_copy(i, who).start()
    for i, who in enumerate((beside, across, diagonal)):
        stat_copy(i, who).wait_recv()
    total = (stat[0] + stat[1]) + (stat[2] + stat[3])

    def column(i):
        return total[:, i : i + 1]

    inv_root = lax.rsqrt(column(0) / D + epsilon)
    weighted_uu = column(1)
    resid_u = inv_root * weighted_uu - column(2)
    sums = jnp.zeros((1, 128), f32)
    pairs = jnp.zeros((1, 128), f32)
    curves = []
    for k in range(2):
        m = [column(3 + k * 8 + i) for i in range(8)]
        curve = slot_curvature(
            inv_root, m[:5], weighted_uu, inv_root * m[5] - m[6], inv_root * m[4] - m[7], resid_u
        )
        curves.append(jnp.sum(jnp.where(eye_tok, curve, 0.0), axis=0, keepdims=True))
        member = ones_where(iota((TOK, 128), 1).astype(f32) == id_col[k])
        sums = sums + jnp.sum(member * curve, axis=0, keepdims=True)
        pairs = pairs + jnp.sum(member, axis=0, keepdims=True)
    row = iota((8, 128), 0)
    est_core[core] = jnp.where(row == 0, sums, jnp.where(row == 1, pairs, 0.0))
    core_copy = pltpu.make_async_remote_copy(
        src_ref=est_core.at[core], dst_ref=est_core.at[core], send_sem=c_send, recv_sem=c_recv, device_id=sibling
    )
    core_copy.start()
    core_copy.wait_recv()
    est_all[chip] = est_core[0] + est_core[1]

    def all_copy(delta):
        return pltpu.make_async_remote_copy(
            src_ref=est_all.at[chip], dst_ref=est_all.at[chip], send_sem=a_send.at[delta], recv_sem=a_recv.at[delta],
            device_id=at((chip + delta) % 16),
        )

    def start_all(delta, _):
        all_copy(delta).start()
        return 0

    lax.fori_loop(1, 16, start_all, 0)
    for block in range(TOK // 16):
        at_ = slice(block * 16, (block + 1) * 16)
        normed_ref[at_] = (gain_ref[...] * usum[at_] * inv_root[at_]).astype(bf16)

    for j in range(PLANES):
        end_dispatch(j)
        passed_on(j).wait_send()
        for unit in (OWN, OTHER):
            for i in range(3):
                exchange(j, unit, i).wait_send()
        to_sibling(j).wait_send()

        def gone(q, _):
            mine, _, there = give(j, q)

            @pl.when(jnp.logical_not(mine))
            def _():
                there.wait_send()

            return 0

        lax.fori_loop(0, 4, gone, 0)
    value_copy.wait_send()
    tangent_copy.wait_send()
    for i, who in enumerate((beside, across, diagonal)):
        stat_copy(i, who).wait_send()
    core_copy.wait_send()

    def end_all(delta, _):
        all_copy(delta).wait()
        return 0

    lax.fori_loop(1, 16, end_all, 0)
    final = jnp.sum(est_all[...], axis=0)
    small_ref[0:2, 0:TOK] = jnp.concatenate(curves, axis=0)
    small_ref[2:3, :] = final[0:1] / jnp.maximum(final[1:2], 1.0)


def deliver(normed_in, small_in, normed_ref, curv_ref, est_ref):
    normed_ref[...] = normed_in[...]
    curv_ref[...] = small_in[0:2, 0:TOK]
    est_ref[...] = small_in[2:3, 0:EXPERTS]


def on_device(tokens, targets, norm_gain, expert_ids, gate_prob, w_gate, gate_probe, w_up, w_down):
    vmem = pl.BlockSpec(memory_space=pltpu.VMEM)
    anywhere = pl.BlockSpec(memory_space=pl.ANY)
    dma = pltpu.SemaphoreType.DMA
    normed, small = pl.pallas_call(
        kernel,
        out_shape=(
            jax.ShapeDtypeStruct((TOK, WIDTH), bf16),
            jax.ShapeDtypeStruct((8, 128), f32),
        ),
        in_specs=[vmem] * 5 + [anywhere] * 4,
        out_specs=(vmem, vmem),
        scratch_shapes=[
            pltpu.VMEM((6, WIDTH, HALF), bf16),
            pltpu.VMEM((HIDDEN, WIDTH), bf16),
            pltpu.VMEM((EXPERTS, MAIN, BLOCK), bf16),
            pltpu.VMEM((PLANES, 2, 4, MAIN, BLOCK), bf16),
            pltpu.VMEM((ROWS, WIDTH), bf16),
            pltpu.VMEM((PLANES, 3, ROWS, HIDDEN), bf16),
            pltpu.VMEM((PLANES, 3, ROWS, HIDDEN), bf16),
            pltpu.VMEM((3 * ROWS, HIDDEN), bf16),
            pltpu.VMEM((3, 128, PIECE), bf16),
            pltpu.VMEM((PLANES, 2, 4, 3, MAIN, BLOCK), bf16),
            pltpu.VMEM((PLANES, 4, 3, MAIN, BLOCK), bf16),
            pltpu.VMEM((PLANES, 4, 3, MAIN, BLOCK), bf16),
            pltpu.VMEM((TOK, WIDTH), bf16),
            pltpu.VMEM((TOK, WIDTH), bf16),
            pltpu.VMEM((2, 2 * TOK, WIDTH // 2), f32),
            pltpu.VMEM((2, 2 * TOK, WIDTH // 2), bf16),
            pltpu.VMEM((2 * TOK, WIDTH // 2), bf16),
            pltpu.VMEM((2 * TOK, WIDTH), f32),
            pltpu.VMEM((TOK, WIDTH), f32),
            pltpu.VMEM((4, TOK, 128), f32),
            pltpu.VMEM((2, 8, 128), f32),
            pltpu.VMEM((16, 8, 128), f32),
            dma((7,)),
            dma((PLANES, 4)), dma((PLANES, 4)),
            dma((PLANES,)), dma((PLANES,)),
            dma((PLANES, 2, 3)), dma((PLANES, 2, 3)),
            dma((PLANES,)), dma((PLANES,)),
            dma((PLANES, 4)), dma((PLANES, 4)),
            dma((2,)), dma((2,)),
            dma((3,)), dma((3,)),
            dma, dma,
            dma((16,)), dma((16,)),
        ],
        compiler_params=pltpu.CompilerParams(
            collective_id=0, has_side_effects=True, vmem_limit_bytes=60 * 1024 * 1024
        ),
    )(
        expert_ids.T,
        gate_prob.T,
        norm_gain.reshape(1, WIDTH),
        tokens,
        targets,
        w_gate,
        gate_probe,
        w_up,
        w_down,
    )
    normed, curvature, estimate = pl.pallas_call(
        deliver,
        out_shape=(
            jax.ShapeDtypeStruct((TOK, WIDTH), bf16),
            jax.ShapeDtypeStruct((2, TOK), f32),
            jax.ShapeDtypeStruct((1, EXPERTS), f32),
        ),
        in_specs=[vmem, vmem],
        out_specs=(vmem, vmem, vmem),
    )(normed, small)
    return normed, curvature.T, estimate.reshape(EXPERTS)


def solution(mesh):
    return jax.shard_map(
        on_device,
        mesh=mesh,
        in_specs=(
            P("dp", "tensor"),
            P("dp", "tensor"),
            P("tensor"),
            P("dp", None),
            P("dp", None),
            P("tensor", ("dp", "expert")),
            P("tensor", ("dp", "expert")),
            P("tensor", ("dp", "expert")),
            P(("dp", "expert"), "tensor"),
        ),
        out_specs=(P("dp", "tensor"), P("dp", None), P()),
        check_vma=False,
    )
```

```python
import functools

import jax
import jax.numpy as jnp
from jax import lax
from jax.experimental import pallas as pl
from jax.experimental.pallas import tpu as pltpu
from jax.sharding import PartitionSpec as P

D = 4096
EXPERTS = 8
TOK = 64
CAP = 18
MAIN = 16
FOLD = 8
PLANES = 4
OWNERS = 8
ROWS = OWNERS * CAP
WIDTH = 2048
PIECE = WIDTH // FOLD
BLOCK = WIDTH + PIECE
HIDDEN = 1024
HALF = HIDDEN // 2
OWN = (0, 64)
OTHER = (64, 80)

epsilon = 1e-05
loss_weight = 8.0
bf16 = jnp.bfloat16
f32 = jnp.float32


def iota(shape, dim):
    return lax.broadcasted_iota(jnp.int32, shape, dim)


def ones_where(mask):
    return jnp.where(mask, 1.0, 0.0).astype(f32)


def dot(a, b):
    return jnp.dot(a, b, preferred_element_type=f32)


def slot_curvature(inv_root, moments, weighted_uu, resid_b, resid_a, resid_u):
    inv_cube = inv_root * inv_root * inv_root
    first_rate = 2.0 * moments[0] / D
    second_rate = 2.0 * (moments[1] + moments[2]) / D
    slope_one = -0.5 * inv_cube * first_rate
    slope_two = (
        0.75 * inv_cube * inv_root * inv_root * first_rate * first_rate
        - 0.5 * inv_cube * second_rate
    )
    tangent_sq = (
        inv_root * inv_root * moments[3]
        + 2.0 * inv_root * slope_one * moments[4]
        + slope_one * slope_one * weighted_uu
    )
    bending = inv_root * resid_b + 2.0 * slope_one * resid_a + slope_two * resid_u
    return 2.0 * loss_weight / D * (tangent_sq + bending)


def kernel(
    ids_ref, prob_ref, gain_ref, tokens_ref, targets_ref, wg_hbm, wp_hbm, wu_hbm, wd_hbm,
    normed_ref, small_ref,
    w_in, w_down, out_rows, rows, lhs, tsend, trecv, jets, folded, img, sib, ret,
    pown, prec, aown, asend, arec, bown, usum, stat, est_core, est_all,
    w_sem, d_send, d_recv, f_send, f_recv, t_send, t_recv, s_send, s_recv, r_send, r_recv,
    e_send, e_recv, st_send, st_recv, c_send, c_recv, a_send, a_recv,
):
    dp = lax.axis_index("dp")
    x_half = lax.axis_index("expert")
    part = lax.axis_index("tensor")
    z, y, core = dp // 8, (dp // 2) % 4, dp % 2
    chip = dp // 2
    sibling = {"dp": chip * 2 + (1 - core)}
    beside = {"tensor": 1 - part}
    across = {"expert": 1 - x_half}
    diagonal = {"expert": 1 - x_half, "tensor": 1 - part}

    def at(chip_index):
        return {"dp": chip_index * 2 + core}

    barrier = pltpu.get_barrier_semaphore()
    for who in (sibling, beside, across, diagonal):
        pl.semaphore_signal(barrier, inc=1, device_id=who)

    def greet(delta, _):
        pl.semaphore_signal(barrier, inc=1, device_id=at((chip + delta) % 16))
        return 0

    lax.fori_loop(1, 16, greet, 0)

    def weights(i):
        src = (wg_hbm, wp_hbm, wu_hbm)[i // 2].at[:, pl.ds((i % 2) * HALF, HALF)]
        return pltpu.make_async_copy(src, w_in.at[i], w_sem.at[i])

    for i in range(6):
        weights(i).start()
    down = pltpu.make_async_copy(wd_hbm, w_down, w_sem.at[6])
    down.start()

    ids = ids_ref[...]
    names = (ids[0:1, :] == iota((EXPERTS, TOK), 0)) | (ids[1:2, :] == iota((EXPERTS, TOK), 0))
    names = ones_where(names).astype(bf16)
    before = ones_where(iota((TOK, TOK), 0) < iota((TOK, TOK), 1)).astype(bf16)
    count = dot(names, before).astype(bf16)
    spread = ones_where((iota((128, EXPERTS), 0) >> 4) == iota((128, EXPERTS), 1)).astype(bf16)
    slot_of = dot(spread, count).astype(jnp.int32)
    named = dot(spread, names) > 0.5
    line = iota((128, TOK), 0)
    pick_main = ones_where(named & (slot_of == (line & 15))).astype(bf16)
    pick_fold = named & (slot_of == MAIN + (line & 1))
    out_rows[:, :, :WIDTH] = dot(pick_main, tokens_ref[...]).astype(bf16).reshape(EXPERTS, MAIN, WIDTH)
    fold = jnp.zeros((128, PIECE), f32)
    for f in range(FOLD):
        pick = ones_where(pick_fold & (((line >> 1) & 7) == f)).astype(bf16)
        fold = fold + dot(pick, tokens_ref[:, f * PIECE : (f + 1) * PIECE])
    out_rows[:, :, WIDTH:] = fold.astype(bf16).reshape(EXPERTS, MAIN, PIECE)

    pl.semaphore_wait(barrier, 19)

    def plane_of(j, q):
        return (z + (j + y + q) % PLANES) % PLANES

    def dispatch(j, q):
        target = plane_of(j, q) * 4 + q
        block = out_rows.at[plane_of(j, q) * 2 + q // 2]
        here = pltpu.make_async_copy(block, rows.at[j, core, y], d_recv.at[j, y])
        there = pltpu.make_async_remote_copy(
            src_ref=block, dst_ref=rows.at[j, core, y], send_sem=d_send.at[j, q], recv_sem=d_recv.at[j, y],
            device_id=at(target),
        )
        return target == chip, here, there

    def start_dispatch(j):
        def one(q, _):
            mine, here, there = dispatch(j, q)

            @pl.when(mine)
            def _():
                here.start()

            @pl.when(jnp.logical_not(mine))
            def _():
                there.start()

            return 0

        lax.fori_loop(0, 4, one, 0)

    def end_dispatch(j):
        def one(q, _):
            mine, _, there = dispatch(j, q)

            @pl.when(jnp.logical_not(mine))
            def _():
                there.wait_send()

            return 0

        lax.fori_loop(0, 4, one, 0)

    def passed_on(j):
        return pltpu.make_async_remote_copy(
            src_ref=rows.at[j, core], dst_ref=rows.at[j, core], send_sem=f_send.at[j], recv_sem=f_recv.at[j],
            device_id=sibling,
        )

    def arrive(j):
        def one(q, _):
            pltpu.make_async_copy(out_rows.at[0], rows.at[j, core, q], d_recv.at[j, q]).wait()
            return 0

        lax.fori_loop(0, 4, one, 0)
        passed_on(j).start()

    a_, b_ = iota((128, 128), 0), iota((128, 128), 1)
    swap = ones_where(
        ((a_ >> 4) == ((b_ >> 1) & 7)) & (((a_ >> 1) & 7) == (b_ >> 4)) & ((a_ & 1) == (b_ & 1))
    ).astype(bf16)

    def exchange(j, unit, i):
        at_ = pl.ds(*unit)
        number = 0 if unit == OWN else 1
        return pltpu.make_async_remote_copy(
            src_ref=tsend.at[j, i, at_], dst_ref=trecv.at[j, i, at_],
            send_sem=t_send.at[j, number, i], recv_sem=t_recv.at[j, number, i], device_id=beside,
        )

    def project(j, unit, send):
        first, many = unit
        at_ = slice(first, first + many)
        if unit == OWN:
            lhs[at_, :] = rows[j, core, :, :, :WIDTH].reshape(64, WIDTH)
        else:
            passed_on(j).wait_recv()
            lhs[64:128, :] = rows[j, 1 - core, :, :, :WIDTH].reshape(64, WIDTH)
            extra = rows[j, :, :, :, WIDTH:].reshape(128, PIECE)
            extra = dot(swap, extra).astype(bf16)
            for f in range(FOLD):
                lhs[128:, f * PIECE : (f + 1) * PIECE] = extra[f * 16 : (f + 1) * 16]

        def one(i, _):
            for half in range(2):
                w = i * 2 + half
                if j == 0 and unit == OWN:
                    pltpu.make_async_copy(w_in.at[w], w_in.at[w], w_sem.at[w]).wait()
                tsend[j, i, at_, half * HALF : (half + 1) * HALF] = dot(lhs[at_, :], w_in[w]).astype(bf16)
            if send:
                exchange(j, unit, i).start()
            return 0

        lax.fori_loop(0, 3, one, 0)

    def to_sibling(j):
        return pltpu.make_async_remote_copy(
            src_ref=img.at[j, 1 - core], dst_ref=sib.at[j], send_sem=s_send.at[j], recv_sem=s_recv.at[j],
            device_id=sibling,
        )

    def expand(j, unit, following):
        first, many = unit
        for i in range(3):
            exchange(j, unit, i).wait_recv()
        if following:
            for i in range(3):
                exchange(*following, i).start()

        def one(block, _):
            at_ = pl.ds(pl.multiple_of(first + block * 16, 16), 16)

            def pre(i):
                return tsend[j, i, at_].astype(f32) + trecv[j, i, at_].astype(f32)

            g, d, u = pre(0), pre(1), pre(2)
            s = jax.nn.sigmoid(g)
            slope = s * (1.0 + g * (1.0 - s))
            second = s * (1.0 - s) * (2.0 + g * (1.0 - 2.0 * s))
            jets[pl.ds(pl.multiple_of(block * 16, 16), 16)] = (g * s * u).astype(bf16)
            jets[pl.ds(pl.multiple_of(many + block * 16, 16), 16)] = (slope * d * u).astype(bf16)
            jets[pl.ds(pl.multiple_of(2 * many + block * 16, 16), 16)] = (second * d * d * u).astype(bf16)
            return 0

        lax.fori_loop(0, many // 16, one, 0)
        if j == 0 and unit == OWN:
            down.wait()
        whose = core if unit == OWN else 1 - core

        def piece(n, _):
            cols = pl.ds(pl.multiple_of(n * PIECE, PIECE), PIECE)
            out = dot(jets[: 3 * many], w_down[:, cols]).astype(bf16)
            for i in range(3):
                top = i * many
                img[j, whose, :, i, :, cols] = out[top : top + 64].reshape(4, MAIN, PIECE)
                if unit != OWN:
                    folded[i, pl.ds(pl.multiple_of(n * 16, 16), 16)] = out[top + 64 : top + 80]
            return 0

        lax.fori_loop(0, FOLD, piece, 0)
        if unit != OWN:
            for i in range(3):
                extra = dot(swap, folded[i]).astype(bf16)
                img[j, :, :, i, :, WIDTH:] = extra.reshape(2, 4, MAIN, PIECE)
            to_sibling(j).start()

    def give(j, q):
        target = ((z + PLANES - (j + y + q) % PLANES) % PLANES) * 4 + q
        here = pltpu.make_async_copy(img.at[j, core, q], ret.at[j, y], r_recv.at[j, y])
        there = pltpu.make_async_remote_copy(
            src_ref=img.at[j, core, q], dst_ref=ret.at[j, y], send_sem=r_send.at[j, q], recv_sem=r_recv.at[j, y],
            device_id=at(target),
        )
        return target == chip, here, there

    def give_back(j):
        to_sibling(j).wait_recv()

        def one(q, _):
            img[j, core, q] = (img[j, core, q].astype(f32) + sib[j, q].astype(f32)).astype(bf16)
            mine, here, there = give(j, q)

            @pl.when(mine)
            def _():
                here.start()

            @pl.when(jnp.logical_not(mine))
            def _():
                there.start()

            return 0

        lax.fori_loop(0, 4, one, 0)

    units = [(0, OWN), (0, OTHER)] + [(j, unit) for j in range(1, PLANES) for unit in (OTHER, OWN)]
    start_dispatch(0)
    arrive(0)
    project(*units[0], True)
    for j in range(1, PLANES):
        start_dispatch(j)
    project(*units[1], True)
    arrive(1)
    project(*units[2], False)
    arrive(2)
    arrive(3)
    for n, (j, unit) in enumerate(units):
        expand(j, unit, units[n + 2] if n + 2 < len(units) else None)
        if n + 3 < len(units):
            project(*units[n + 3], False)
        if n == 2:
            give_back(0)
        if j > 0 and unit == OWN:
            give_back(j)

    line = iota((256, TOK), 0)
    plane = (z + (((line >> 6) + (line >> 4) + y) & 3)) & 3
    expert_of = plane * 2 + ((line >> 5) & 1)
    small = iota((256, EXPERTS), 0)
    small = ((z + (((small >> 6) + (small >> 4) + y) & 3)) & 3) * 2 + ((small >> 5) & 1)
    spread_back = ones_where(small == iota((256, EXPERTS), 1)).astype(bf16)
    slot_back = dot(spread_back, count).astype(jnp.int32)
    eye_tok = iota((TOK, TOK), 0) == iota((TOK, TOK), 1)

    def upright(row):
        return jnp.sum(jnp.where(eye_tok, row, 0.0), axis=1, keepdims=True)

    def for_ids(make):
        return jnp.concatenate([make(ids[k : k + 1, :]) for k in range(2)], axis=0)

    back_main = for_ids(lambda row: ones_where((expert_of == row) & (slot_back == (line & 15))).T).astype(bf16)
    back_fold = for_ids(lambda row: ones_where((expert_of == row) & (slot_back == MAIN + (line & 1))).T)
    fold_index = (iota((2 * TOK, 256), 1) >> 1) & 7
    prob_col = jnp.concatenate([upright(prob_ref[k : k + 1, :]) for k in range(2)], axis=0)
    id_col = [upright(ids[k : k + 1, :].astype(f32)) for k in range(2)]

    for j in range(PLANES):
        for q in range(4):
            pltpu.make_async_copy(ret.at[j, q], ret.at[j, q], r_recv.at[j, q]).wait()

    def picked(i, f):
        pick = jnp.where(fold_index == f, back_fold, 0.0).astype(bf16)
        whole = ret[:, :, i, :, pl.ds(pl.multiple_of(f * PIECE, PIECE), PIECE)].reshape(256, PIECE)
        extra = ret[:, :, i, :, WIDTH:].reshape(256, PIECE)
        return prob_col * (dot(back_main, whole) + dot(pick, extra))

    def values(f, _):
        value = picked(0, f)
        pown[:, pl.ds(pl.multiple_of(f * PIECE, PIECE), PIECE)] = (value[:TOK] + value[TOK:]).astype(bf16)
        return 0

    def tangents(f, _):
        half_cols = pl.ds(pl.multiple_of((f % 4) * PIECE, PIECE), PIECE)
        tangent = picked(1, f)
        aown[f // 4, :, half_cols] = tangent
        asend[f // 4, :, half_cols] = tangent.astype(bf16)
        return 0

    def seconds(f, _):
        bown[:, pl.ds(pl.multiple_of(f * PIECE, PIECE), PIECE)] = picked(2, f)
        return 0

    value_copy = pltpu.make_async_remote_copy(
        src_ref=pown, dst_ref=prec, send_sem=e_send.at[0], recv_sem=e_recv.at[0], device_id=across
    )
    tangent_copy = pltpu.make_async_remote_copy(
        src_ref=asend.at[1 - x_half], dst_ref=arec, send_sem=e_send.at[1], recv_sem=e_recv.at[1], device_id=across
    )
    lax.fori_loop(0, FOLD, values, 0)
    value_copy.start()
    lax.fori_loop(0, FOLD, tangents, 0)
    tangent_copy.start()
    lax.fori_loop(0, FOLD, seconds, 0)

    me = x_half * 2 + part
    lane = iota((16, 128), 1)
    near = pl.ds(pl.multiple_of(x_half * (WIDTH // 2), WIDTH // 2), WIDTH // 2)

    def over(v):
        return jnp.sum(v, axis=-1, keepdims=True)

    def lay(values, laid):
        for i, value in values.items():
            laid = jnp.where(lane == i, value, laid)
        return laid

    def inner_value(block, _):
        at_ = pl.ds(pl.multiple_of(block * 16, 16), 16)
        u = tokens_ref[at_].astype(f32) + (pown[at_].astype(f32) + prec[at_].astype(f32))
        usum[at_] = u
        gain = gain_ref[...]
        heavy = gain * gain * u
        goal = gain * targets_ref[at_].astype(f32)
        stats = {}
        for k in range(2):
            b = bown[pl.ds(pl.multiple_of(k * TOK + block * 16, 16), 16)]
            stats[3 + k * 8 + 2] = over(u * b)
            stats[3 + k * 8 + 5] = over(heavy * b)
            stats[3 + k * 8 + 6] = over(goal * b)
        gain = gain_ref[:, near]
        u = usum[at_, near]
        heavy = gain * gain * u
        goal = gain * targets_ref[at_, near].astype(f32)
        stats[0] = over(u * u)
        stats[1] = over(heavy * u)
        stats[2] = over(goal * u)
        stat[me, at_] = lay(stats, jnp.zeros((16, 128), f32))
        return 0

    def inner_tangent(block, _):
        at_ = pl.ds(pl.multiple_of(block * 16, 16), 16)
        gain = gain_ref[:, near]
        u = usum[at_, near]
        heavy = gain * gain * u
        goal = gain * targets_ref[at_, near].astype(f32)
        stats = {}
        for k in range(2):
            own = pl.ds(pl.multiple_of(k * TOK + block * 16, 16), 16)
            a = aown[x_half, own] + arec[own].astype(f32)
            stats[3 + k * 8 + 0] = over(u * a)
            stats[3 + k * 8 + 1] = over(a * a)
            stats[3 + k * 8 + 3] = over(gain * gain * a * a)
            stats[3 + k * 8 + 4] = over(heavy * a)
            stats[3 + k * 8 + 7] = over(goal * a)
        stat[me, at_] = lay(stats, stat[me, at_])
        return 0

    value_copy.wait_recv()
    lax.fori_loop(0, TOK // 16, inner_value, 0)
    tangent_copy.wait_recv()
    lax.fori_loop(0, TOK // 16, inner_tangent, 0)

    def stat_copy(i, who):
        return pltpu.make_async_remote_copy(
            src_ref=stat.at[me], dst_ref=stat.at[me], send_sem=st_send.at[i], recv_sem=st_recv.at[i], device_id=who
        )

    for i, who in enumerate((beside, across, diagonal)):
        stat_copy(i, who).start()
    for i, who in enumerate((beside, across, diagonal)):
        stat_copy(i, who).wait_recv()
    total = (stat[0] + stat[1]) + (stat[2] + stat[3])

    def column(i):
        return total[:, i : i + 1]

    inv_root = lax.rsqrt(column(0) / D + epsilon)
    weighted_uu = column(1)
    resid_u = inv_root * weighted_uu - column(2)
    sums = jnp.zeros((1, 128), f32)
    pairs = jnp.zeros((1, 128), f32)
    curves = []
    for k in range(2):
        m = [column(3 + k * 8 + i) for i in range(8)]
        curve = slot_curvature(
            inv_root, m[:5], weighted_uu, inv_root * m[5] - m[6], inv_root * m[4] - m[7], resid_u
        )
        curves.append(jnp.sum(jnp.where(eye_tok, curve, 0.0), axis=0, keepdims=True))
        member = ones_where(iota((TOK, 128), 1).astype(f32) == id_col[k])
        sums = sums + jnp.sum(member * curve, axis=0, keepdims=True)
        pairs = pairs + jnp.sum(member, axis=0, keepdims=True)
    row = iota((8, 128), 0)
    est_core[core] = jnp.where(row == 0, sums, jnp.where(row == 1, pairs, 0.0))
    core_copy = pltpu.make_async_remote_copy(
        src_ref=est_core.at[core], dst_ref=est_core.at[core], send_sem=c_send, recv_sem=c_recv, device_id=sibling
    )
    core_copy.start()
    core_copy.wait_recv()
    est_all[chip] = est_core[0] + est_core[1]

    def all_copy(delta):
        return pltpu.make_async_remote_copy(
            src_ref=est_all.at[chip], dst_ref=est_all.at[chip], send_sem=a_send.at[delta], recv_sem=a_recv.at[delta],
            device_id=at((chip + delta) % 16),
        )

    def start_all(delta, _):
        all_copy(delta).start()
        return 0

    lax.fori_loop(1, 16, start_all, 0)
    for block in range(TOK // 16):
        at_ = slice(block * 16, (block + 1) * 16)
        normed_ref[at_] = (gain_ref[...] * usum[at_] * inv_root[at_]).astype(bf16)

    for j in range(PLANES):
        end_dispatch(j)
        passed_on(j).wait_send()
        for unit in (OWN, OTHER):
            for i in range(3):
                exchange(j, unit, i).wait_send()
        to_sibling(j).wait_send()

        def gone(q, _):
            mine, _, there = give(j, q)

            @pl.when(jnp.logical_not(mine))
            def _():
                there.wait_send()

            return 0

        lax.fori_loop(0, 4, gone, 0)
    value_copy.wait_send()
    tangent_copy.wait_send()
    for i, who in enumerate((beside, across, diagonal)):
        stat_copy(i, who).wait_send()
    core_copy.wait_send()

    def end_all(delta, _):
        all_copy(delta).wait()
        return 0

    lax.fori_loop(1, 16, end_all, 0)
    final = jnp.sum(est_all[...], axis=0)
    small_ref[0:2, 0:TOK] = jnp.concatenate(curves, axis=0)
    small_ref[2:3, :] = final[0:1] / jnp.maximum(final[1:2], 1.0)


def deliver(normed_in, small_in, normed_ref, curv_ref, est_ref):
    normed_ref[...] = normed_in[...]
    curv_ref[...] = small_in[0:2, 0:TOK]
    est_ref[...] = small_in[2:3, 0:EXPERTS]


def on_device(tokens, targets, norm_gain, expert_ids, gate_prob, w_gate, gate_probe, w_up, w_down):
    vmem = pl.BlockSpec(memory_space=pltpu.VMEM)
    anywhere = pl.BlockSpec(memory_space=pl.ANY)
    dma = pltpu.SemaphoreType.DMA
    normed, small = pl.pallas_call(
        kernel,
        out_shape=(
            jax.ShapeDtypeStruct((TOK, WIDTH), bf16),
            jax.ShapeDtypeStruct((8, 128), f32),
        ),
        in_specs=[vmem] * 5 + [anywhere] * 4,
        out_specs=(vmem, vmem),
        scratch_shapes=[
            pltpu.VMEM((6, WIDTH, HALF), bf16),
            pltpu.VMEM((HIDDEN, WIDTH), bf16),
            pltpu.VMEM((EXPERTS, MAIN, BLOCK), bf16),
            pltpu.VMEM((PLANES, 2, 4, MAIN, BLOCK), bf16),
            pltpu.VMEM((ROWS, WIDTH), bf16),
            pltpu.VMEM((PLANES, 3, ROWS, HIDDEN), bf16),
            pltpu.VMEM((PLANES, 3, ROWS, HIDDEN), bf16),
            pltpu.VMEM((3 * ROWS, HIDDEN), bf16),
            pltpu.VMEM((3, 128, PIECE), bf16),
            pltpu.VMEM((PLANES, 2, 4, 3, MAIN, BLOCK), bf16),
            pltpu.VMEM((PLANES, 4, 3, MAIN, BLOCK), bf16),
            pltpu.VMEM((PLANES, 4, 3, MAIN, BLOCK), bf16),
            pltpu.VMEM((TOK, WIDTH), bf16),
            pltpu.VMEM((TOK, WIDTH), bf16),
            pltpu.VMEM((2, 2 * TOK, WIDTH // 2), f32),
            pltpu.VMEM((2, 2 * TOK, WIDTH // 2), bf16),
            pltpu.VMEM((2 * TOK, WIDTH // 2), bf16),
            pltpu.VMEM((2 * TOK, WIDTH), f32),
            pltpu.VMEM((TOK, WIDTH), f32),
            pltpu.VMEM((4, TOK, 128), f32),
            pltpu.VMEM((2, 8, 128), f32),
            pltpu.VMEM((16, 8, 128), f32),
            dma((7,)),
            dma((PLANES, 4)), dma((PLANES, 4)),
            dma((PLANES,)), dma((PLANES,)),
            dma((PLANES, 2, 3)), dma((PLANES, 2, 3)),
            dma((PLANES,)), dma((PLANES,)),
            dma((PLANES, 4)), dma((PLANES, 4)),
            dma((2,)), dma((2,)),
            dma((3,)), dma((3,)),
            dma, dma,
            dma((16,)), dma((16,)),
        ],
        compiler_params=pltpu.CompilerParams(
            collective_id=0, has_side_effects=True, vmem_limit_bytes=60 * 1024 * 1024
        ),
    )(
        expert_ids.T,
        gate_prob.T,
        norm_gain.reshape(1, WIDTH),
        tokens,
        targets,
        w_gate,
        gate_probe,
        w_up,
        w_down,
    )
    normed, curvature, estimate = pl.pallas_call(
        deliver,
        out_shape=(
            jax.ShapeDtypeStruct((TOK, WIDTH), bf16),
            jax.ShapeDtypeStruct((2, TOK), f32),
            jax.ShapeDtypeStruct((1, EXPERTS), f32),
        ),
        in_specs=[vmem, vmem],
        out_specs=(vmem, vmem, vmem),
    )(normed, small)
    return normed, curvature.T, estimate.reshape(EXPERTS)


def solution(mesh):
    return jax.shard_map(
        on_device,
        mesh=mesh,
        in_specs=(
            P("dp", "tensor"),
            P("dp", "tensor"),
            P("tensor"),
            P("dp", None),
            P("dp", None),
            P("tensor", ("dp", "expert")),
            P("tensor", ("dp", "expert")),
            P("tensor", ("dp", "expert")),
            P(("dp", "expert"), "tensor"),
        ),
        out_specs=(P("dp", "tensor"), P("dp", None), P()),
        check_vma=False,
    )
```

```python
import functools

import jax
import jax.numpy as jnp
from jax import lax
from jax.experimental import pallas as pl
from jax.experimental.pallas import tpu as pltpu
from jax.sharding import PartitionSpec as P

D = 4096
EXPERTS = 8
TOK = 64
CAP = 18
MAIN = 16
FOLD = 8
PLANES = 4
OWNERS = 8
ROWS = OWNERS * CAP
WIDTH = 2048
PIECE = WIDTH // FOLD
BLOCK = WIDTH + PIECE
HIDDEN = 1024
HALF = HIDDEN // 2
OWN = (0, 64)
OTHER = (64, 80)
OWN_A = (0, 32)
OWN_B = (32, 32)
UNITS = [(0, OWN), (0, OTHER), (1, OTHER), (1, OWN), (2, OTHER), (2, OWN), (3, OTHER), (3, OWN_A), (3, OWN_B)]

epsilon = 1e-05
loss_weight = 8.0
bf16 = jnp.bfloat16
f32 = jnp.float32


def iota(shape, dim):
    return lax.broadcasted_iota(jnp.int32, shape, dim)


def ones_where(mask):
    return jnp.where(mask, 1.0, 0.0).astype(f32)


def dot(a, b):
    return jnp.dot(a, b, preferred_element_type=f32)


def slot_curvature(inv_root, moments, weighted_uu, resid_b, resid_a, resid_u):
    inv_cube = inv_root * inv_root * inv_root
    first_rate = 2.0 * moments[0] / D
    second_rate = 2.0 * (moments[1] + moments[2]) / D
    slope_one = -0.5 * inv_cube * first_rate
    slope_two = (
        0.75 * inv_cube * inv_root * inv_root * first_rate * first_rate
        - 0.5 * inv_cube * second_rate
    )
    tangent_sq = (
        inv_root * inv_root * moments[3]
        + 2.0 * inv_root * slope_one * moments[4]
        + slope_one * slope_one * weighted_uu
    )
    bending = inv_root * resid_b + 2.0 * slope_one * resid_a + slope_two * resid_u
    return 2.0 * loss_weight / D * (tangent_sq + bending)


def kernel(
    ids_ref, prob_ref, gain_ref, tokens_ref, targets_ref, wg_hbm, wp_hbm, wu_hbm, wd_hbm,
    normed_ref, small_ref,
    w_in, w_down, out_rows, rows, lhs, tsend, trecv, jets, folded, img, sib, ret,
    pown, prec, aown, asend, arec, bown, usum, slot_value, slot_tangent, tangent_out, stat, est_core, est_all,
    w_sem, d_send, d_recv, f_send, f_recv, t_send, t_recv, s_send, s_recv, r_send, r_recv,
    e_send, e_recv, st_send, st_recv, c_send, c_recv, a_send, a_recv,
):
    dp = lax.axis_index("dp")
    x_half = lax.axis_index("expert")
    part = lax.axis_index("tensor")
    z, y, core = dp // 8, (dp // 2) % 4, dp % 2
    chip = dp // 2
    sibling = {"dp": chip * 2 + (1 - core)}
    beside = {"tensor": 1 - part}
    across = {"expert": 1 - x_half}
    diagonal = {"expert": 1 - x_half, "tensor": 1 - part}

    def at(chip_index):
        return {"dp": chip_index * 2 + core}

    barrier = pltpu.get_barrier_semaphore()
    for who in (sibling, beside, across, diagonal):
        pl.semaphore_signal(barrier, inc=1, device_id=who)

    def greet(delta, _):
        pl.semaphore_signal(barrier, inc=1, device_id=at((chip + delta) % 16))
        return 0

    lax.fori_loop(1, 16, greet, 0)

    def weights(i):
        src = (wg_hbm, wp_hbm, wu_hbm)[i // 2].at[:, pl.ds((i % 2) * HALF, HALF)]
        return pltpu.make_async_copy(src, w_in.at[i], w_sem.at[i])

    for i in range(6):
        weights(i).start()
    down = pltpu.make_async_copy(wd_hbm, w_down, w_sem.at[6])
    down.start()

    ids = ids_ref[...]
    names = (ids[0:1, :] == iota((EXPERTS, TOK), 0)) | (ids[1:2, :] == iota((EXPERTS, TOK), 0))
    names = ones_where(names).astype(bf16)
    before = ones_where(iota((TOK, TOK), 0) < iota((TOK, TOK), 1)).astype(bf16)
    count = dot(names, before).astype(bf16)
    spread = ones_where((iota((128, EXPERTS), 0) >> 4) == iota((128, EXPERTS), 1)).astype(bf16)
    slot_of = dot(spread, count).astype(jnp.int32)
    named = dot(spread, names) > 0.5
    line = iota((128, TOK), 0)
    pick_main = ones_where(named & (slot_of == (line & 15))).astype(bf16)
    pick_fold = named & (slot_of == MAIN + (line & 1))
    out_rows[:, :, :WIDTH] = dot(pick_main, tokens_ref[...]).astype(bf16).reshape(EXPERTS, MAIN, WIDTH)
    fold = jnp.zeros((128, PIECE), f32)
    for f in range(FOLD):
        pick = ones_where(pick_fold & (((line >> 1) & 7) == f)).astype(bf16)
        fold = fold + dot(pick, tokens_ref[:, f * PIECE : (f + 1) * PIECE])
    out_rows[:, :, WIDTH:] = fold.astype(bf16).reshape(EXPERTS, MAIN, PIECE)

    pl.semaphore_wait(barrier, 19)

    def plane_of(j, q):
        return (z + (j + y + 2 * (q // 2)) % PLANES) % PLANES

    def dispatch(j, q):
        target = plane_of(j, q) * 4 + q
        block = out_rows.at[plane_of(j, q) * 2 + q // 2]
        here = pltpu.make_async_copy(block, rows.at[j, core, y], d_recv.at[j, y])
        there = pltpu.make_async_remote_copy(
            src_ref=block, dst_ref=rows.at[j, core, y], send_sem=d_send.at[j, q], recv_sem=d_recv.at[j, y],
            device_id=at(target),
        )
        return target == chip, here, there

    def start_dispatch(j):
        def one(q, _):
            mine, here, there = dispatch(j, q)

            @pl.when(mine)
            def _():
                here.start()

            @pl.when(jnp.logical_not(mine))
            def _():
                there.start()

            return 0

        lax.fori_loop(0, 4, one, 0)

    def end_dispatch(j):
        def one(q, _):
            mine, _, there = dispatch(j, q)

            @pl.when(jnp.logical_not(mine))
            def _():
                there.wait_send()

            return 0

        lax.fori_loop(0, 4, one, 0)

    def passed_on(j):
        return pltpu.make_async_remote_copy(
            src_ref=rows.at[j, core], dst_ref=rows.at[j, core], send_sem=f_send.at[j], recv_sem=f_recv.at[j],
            device_id=sibling,
        )

    def arrive(j):
        def one(q, _):
            pltpu.make_async_copy(out_rows.at[0], rows.at[j, core, q], d_recv.at[j, q]).wait()
            return 0

        lax.fori_loop(0, 4, one, 0)
        passed_on(j).start()

    a_, b_ = iota((128, 128), 0), iota((128, 128), 1)
    swap = ones_where(
        ((a_ >> 4) == ((b_ >> 1) & 7)) & (((a_ >> 1) & 7) == (b_ >> 4)) & ((a_ & 1) == (b_ & 1))
    ).astype(bf16)

    def exchange(j, unit, i):
        at_ = pl.ds(*unit)
        number = {OWN: 0, OTHER: 1, OWN_A: 0, OWN_B: 2}[unit]
        return pltpu.make_async_remote_copy(
            src_ref=tsend.at[j, i, at_], dst_ref=trecv.at[j, i, at_],
            send_sem=t_send.at[j, number, i], recv_sem=t_recv.at[j, number, i], device_id=beside,
        )

    def project(j, unit, send):
        first, many = unit
        at_ = slice(first, first + many)
        if unit != OTHER:
            lhs[at_, :] = rows[j, core, first // 16 : (first + many) // 16, :, :WIDTH].reshape(many, WIDTH)
        else:
            passed_on(j).wait_recv()
            lhs[64:128, :] = rows[j, 1 - core, :, :, :WIDTH].reshape(64, WIDTH)
            extra = rows[j, :, :, :, WIDTH:].reshape(128, PIECE)
            extra = dot(swap, extra).astype(bf16)
            for f in range(FOLD):
                lhs[128:, f * PIECE : (f + 1) * PIECE] = extra[f * 16 : (f + 1) * 16]

        def one(i, _):
            for half in range(2):
                w = i * 2 + half
                if j == 0 and unit == OWN:
                    pltpu.make_async_copy(w_in.at[w], w_in.at[w], w_sem.at[w]).wait()
                tsend[j, i, at_, half * HALF : (half + 1) * HALF] = dot(lhs[at_, :], w_in[w]).astype(bf16)
            if send:
                exchange(j, unit, i).start()
            return 0

        lax.fori_loop(0, 3, one, 0)

    def to_sibling(j):
        return pltpu.make_async_remote_copy(
            src_ref=img.at[j, 1 - core], dst_ref=sib.at[j], send_sem=s_send.at[j], recv_sem=s_recv.at[j],
            device_id=sibling,
        )

    def expand(j, unit, following, then=None):
        first, many = unit
        for i in range(3):
            exchange(j, unit, i).wait_recv()
        if following:
            for i in range(3):
                exchange(*following, i).start()
        if then:
            then()

        def one(block, _):
            at_ = pl.ds(pl.multiple_of(first + block * 16, 16), 16)

            def pre(i):
                return tsend[j, i, at_].astype(f32) + trecv[j, i, at_].astype(f32)

            g, d, u = pre(0), pre(1), pre(2)
            s = jax.nn.sigmoid(g)
            slope = s * (1.0 + g * (1.0 - s))
            second = s * (1.0 - s) * (2.0 + g * (1.0 - 2.0 * s))
            jets[pl.ds(pl.multiple_of(block * 16, 16), 16)] = (g * s * u).astype(bf16)
            jets[pl.ds(pl.multiple_of(many + block * 16, 16), 16)] = (slope * d * u).astype(bf16)
            jets[pl.ds(pl.multiple_of(2 * many + block * 16, 16), 16)] = (second * d * d * u).astype(bf16)
            return 0

        lax.fori_loop(0, many // 16, one, 0)
        if j == 0 and unit == OWN:
            down.wait()
        whose = 1 - core if unit == OTHER else core
        places = slice(0, 4) if unit == OTHER else slice(first // 16, (first + many) // 16)
        whole = 64 if unit == OTHER else many

        def piece(n, _):
            cols = pl.ds(pl.multiple_of(n * PIECE, PIECE), PIECE)
            out = dot(jets[: 3 * many], w_down[:, cols]).astype(bf16)
            for i in range(3):
                top = i * many
                img[j, whose, places, i, :, cols] = out[top : top + whole].reshape(whole // 16, MAIN, PIECE)
                if unit == OTHER:
                    folded[i, pl.ds(pl.multiple_of(n * 16, 16), 16)] = out[top + 64 : top + 80]
            return 0

        lax.fori_loop(0, FOLD, piece, 0)
        if unit == OTHER:
            for i in range(3):
                extra = dot(swap, folded[i]).astype(bf16)
                img[j, :, :, i, :, WIDTH:] = extra.reshape(2, 4, MAIN, PIECE)
            to_sibling(j).start()

    def give(j, q):
        target = ((z + PLANES - (j + q + 2 * (y // 2)) % PLANES) % PLANES) * 4 + q
        here = pltpu.make_async_copy(img.at[j, core, q], ret.at[j, y], r_recv.at[j, y])
        there = pltpu.make_async_remote_copy(
            src_ref=img.at[j, core, q], dst_ref=ret.at[j, y], send_sem=r_send.at[j, q], recv_sem=r_recv.at[j, y],
            device_id=at(target),
        )
        return target == chip, here, there

    def give_back(j, low=0, high=4):
        if low == 0:
            to_sibling(j).wait_recv()

        def one(q, _):
            img[j, core, q] = (img[j, core, q].astype(f32) + sib[j, q].astype(f32)).astype(bf16)
            mine, here, there = give(j, q)

            @pl.when(mine)
            def _():
                here.start()

            @pl.when(jnp.logical_not(mine))
            def _():
                there.start()

            return 0

        lax.fori_loop(low, high, one, 0)

    eye_tok = iota((TOK, TOK), 0) == iota((TOK, TOK), 1)

    def upright(row):
        return jnp.sum(jnp.where(eye_tok, row, 0.0), axis=1, keepdims=True)

    prob_col = jnp.concatenate([upright(prob_ref[k : k + 1, :]) for k in range(2)], axis=0)
    id_col = [upright(ids[k : k + 1, :].astype(f32)) for k in range(2)]

    def back(many, place):
        line = iota((many, TOK), 0)

        def expert(line):
            j, pair = place(line)
            return ((z + ((j + y + 2 * pair) & 3)) & 3) * 2 + pair

        spread = ones_where(expert(iota((many, EXPERTS), 0)) == iota((many, EXPERTS), 1)).astype(bf16)
        slot = dot(spread, count).astype(jnp.int32)

        def for_ids(wanted):
            masks = [(expert(line) == ids[k : k + 1, :]) & (slot == wanted) for k in range(2)]
            return jnp.concatenate([ones_where(m).T for m in masks], axis=0)

        return for_ids(line & 15).astype(bf16), for_ids(MAIN + (line & 1)), (iota((2 * TOK, many), 1) >> 1) & 7

    def picked(backs, whole, extra, f):
        main, fold, index = backs
        pick = jnp.where(index == f, fold, 0.0).astype(bf16)
        return prob_col * (dot(main, whole) + dot(pick, extra))

    def across_copy(i, src, dst):
        return pltpu.make_async_remote_copy(
            src_ref=src, dst_ref=dst, send_sem=e_send.at[i], recv_sem=e_recv.at[i], device_id=across
        )

    def early_value():
        return across_copy(0, pown, prec)

    def early_tangent():
        return across_copy(1, asend.at[1 - x_half], arec)

    def late_value():
        return across_copy(2, slot_value.at[x_half], slot_value.at[x_half])

    def late_tangent():
        return across_copy(3, tangent_out, slot_tangent.at[x_half])

    def returned(j):
        for q in range(4):
            pltpu.make_async_copy(ret.at[j, q], ret.at[j, q], r_recv.at[j, q]).wait()

    def early():
        backs = back(64 * (PLANES - 1), lambda line: (line >> 6, (line >> 5) & 1))
        for j in range(PLANES - 1):
            returned(j)

        def piece(f, _):
            cols = pl.ds(pl.multiple_of(f * PIECE, PIECE), PIECE)
            half_cols = pl.ds(pl.multiple_of((f % 4) * PIECE, PIECE), PIECE)

            def of(i):
                whole = ret[: PLANES - 1, :, i, :, cols].reshape(64 * (PLANES - 1), PIECE)
                extra = ret[: PLANES - 1, :, i, :, WIDTH:].reshape(64 * (PLANES - 1), PIECE)
                return picked(backs, whole, extra, f)

            value = of(0)
            pown[:, cols] = (value[:TOK] + value[TOK:]).astype(bf16)
            tangent = of(1)
            aown[f // 4, :, half_cols] = tangent
            asend[f // 4, :, half_cols] = tangent.astype(bf16)
            bown[:, cols] = of(2)
            return 0

        lax.fori_loop(0, FOLD, piece, 0)

    def send_early():
        early_value().start()
        early_tangent().start()

    start_dispatch(0)
    arrive(0)
    project(*UNITS[0], True)
    for j in range(1, PLANES):
        start_dispatch(j)
    project(*UNITS[1], True)
    arrive(1)
    project(*UNITS[2], False)
    arrive(2)
    arrive(3)
    for n, (j, unit) in enumerate(UNITS):
        last = n == len(UNITS) - 1
        expand(j, unit, UNITS[n + 2] if n + 2 < len(UNITS) else None, send_early if last else None)
        if n + 3 < len(UNITS):
            project(*UNITS[n + 3], False)
        if n == 2:
            give_back(0)
        if j > 0 and unit == OWN:
            give_back(j)
        if unit == OWN_A:
            give_back(j, 0, 2)
        if unit == OWN_B:
            give_back(j, 2, 4)
        if (j, unit) == (3, OTHER):
            early()

    final = PLANES - 1
    near = pl.ds(pl.multiple_of(x_half * (WIDTH // 2), WIDTH // 2), WIDTH // 2)
    far = pl.ds(pl.multiple_of((1 - x_half) * (WIDTH // 2), WIDTH // 2), WIDTH // 2)
    late_backs = back(64, lambda line: (final, (line >> 4) & 1))
    second_backs = back(64, lambda line: (final, (line >> 5) & 1))
    returned(final)

    def pair_sum(pair, i, cols):
        both = ret[final, 2 * pair, i, :, cols].astype(f32) + ret[final, 2 * pair + 1, i, :, cols].astype(f32)
        return both.astype(bf16)

    for pair in range(2):
        slot_value[x_half, pair] = pair_sum(pair, 0, slice(0, BLOCK))
    late_value().start()
    for pair in range(2):
        tangent_out[pair, :, : WIDTH // 2] = pair_sum(pair, 1, far)
        tangent_out[pair, :, WIDTH // 2 :] = pair_sum(pair, 1, slice(WIDTH, BLOCK))
    late_tangent().start()
    for pair in range(2):
        slot_tangent[x_half, pair, :, : WIDTH // 2] = pair_sum(pair, 1, near)
        slot_tangent[x_half, pair, :, WIDTH // 2 :] = pair_sum(pair, 1, slice(WIDTH, BLOCK))

    def late_second(f, _):
        cols = pl.ds(pl.multiple_of(f * PIECE, PIECE), PIECE)
        whole = ret[final, :, 2, :, cols].reshape(64, PIECE)
        extra = ret[final, :, 2, :, WIDTH:].reshape(64, PIECE)
        bown[:, cols] += picked(second_backs, whole, extra, f)
        return 0

    lax.fori_loop(0, FOLD, late_second, 0)

    def late_piece(f, _):
        cols = pl.ds(pl.multiple_of(f * PIECE, PIECE), PIECE)
        whole = slot_value[:, :, :, cols].reshape(64, PIECE)
        extra = slot_value[:, :, :, WIDTH:].reshape(64, PIECE)
        value = picked(late_backs, whole, extra, f)
        usum[:, cols] = value[:TOK] + value[TOK:]
        return 0

    def late_slope(f, _):
        cols = pl.ds(pl.multiple_of(f * PIECE, PIECE), PIECE)
        whole = slot_tangent[:, :, :, cols].reshape(64, PIECE)
        extra = slot_tangent[:, :, :, WIDTH // 2 :].reshape(64, PIECE)
        aown[x_half, :, cols] += picked(late_backs, whole, extra, x_half * 4 + f)
        return 0

    me = x_half * 2 + part
    lane = iota((16, 128), 1)

    def over(v):
        return jnp.sum(v, axis=-1, keepdims=True)

    def lay(values, laid):
        for i, value in values.items():
            laid = jnp.where(lane == i, value, laid)
        return laid

    def inner_value(block, _):
        at_ = pl.ds(pl.multiple_of(block * 16, 16), 16)
        u = tokens_ref[at_].astype(f32) + (pown[at_].astype(f32) + prec[at_].astype(f32)) + usum[at_]
        usum[at_] = u
        gain = gain_ref[...]
        heavy = gain * gain * u
        goal = gain * targets_ref[at_].astype(f32)
        stats = {}
        for k in range(2):
            b = bown[pl.ds(pl.multiple_of(k * TOK + block * 16, 16), 16)]
            stats[3 + k * 8 + 2] = over(u * b)
            stats[3 + k * 8 + 5] = over(heavy * b)
            stats[3 + k * 8 + 6] = over(goal * b)
        gain = gain_ref[:, near]
        u = usum[at_, near]
        heavy = gain * gain * u
        goal = gain * targets_ref[at_, near].astype(f32)
        stats[0] = over(u * u)
        stats[1] = over(heavy * u)
        stats[2] = over(goal * u)
        stat[me, at_] = lay(stats, jnp.zeros((16, 128), f32))
        return 0

    def inner_tangent(block, _):
        at_ = pl.ds(pl.multiple_of(block * 16, 16), 16)
        gain = gain_ref[:, near]
        u = usum[at_, near]
        heavy = gain * gain * u
        goal = gain * targets_ref[at_, near].astype(f32)
        stats = {}
        for k in range(2):
            own = pl.ds(pl.multiple_of(k * TOK + block * 16, 16), 16)
            a = aown[x_half, own] + arec[own].astype(f32)
            stats[3 + k * 8 + 0] = over(u * a)
            stats[3 + k * 8 + 1] = over(a * a)
            stats[3 + k * 8 + 3] = over(gain * gain * a * a)
            stats[3 + k * 8 + 4] = over(heavy * a)
            stats[3 + k * 8 + 7] = over(goal * a)
        stat[me, at_] = lay(stats, stat[me, at_])
        return 0

    early_value().wait_recv()
    late_value().wait_recv()
    lax.fori_loop(0, FOLD, late_piece, 0)
    lax.fori_loop(0, TOK // 16, inner_value, 0)
    early_tangent().wait_recv()
    late_tangent().wait_recv()
    lax.fori_loop(0, FOLD // 2, late_slope, 0)
    lax.fori_loop(0, TOK // 16, inner_tangent, 0)

    def stat_copy(i, who):
        return pltpu.make_async_remote_copy(
            src_ref=stat.at[me], dst_ref=stat.at[me], send_sem=st_send.at[i], recv_sem=st_recv.at[i], device_id=who
        )

    for i, who in enumerate((beside, across, diagonal)):
        stat_copy(i, who).start()
    for i, who in enumerate((beside, across, diagonal)):
        stat_copy(i, who).wait_recv()
    total = (stat[0] + stat[1]) + (stat[2] + stat[3])

    def column(i):
        return total[:, i : i + 1]

    inv_root = lax.rsqrt(column(0) / D + epsilon)
    weighted_uu = column(1)
    resid_u = inv_root * weighted_uu - column(2)
    sums = jnp.zeros((1, 128), f32)
    pairs = jnp.zeros((1, 128), f32)
    curves = []
    for k in range(2):
        m = [column(3 + k * 8 + i) for i in range(8)]
        curve = slot_curvature(
            inv_root, m[:5], weighted_uu, inv_root * m[5] - m[6], inv_root * m[4] - m[7], resid_u
        )
        curves.append(jnp.sum(jnp.where(eye_tok, curve, 0.0), axis=0, keepdims=True))
        member = ones_where(iota((TOK, 128), 1).astype(f32) == id_col[k])
        sums = sums + jnp.sum(member * curve, axis=0, keepdims=True)
        pairs = pairs + jnp.sum(member, axis=0, keepdims=True)
    row = iota((8, 128), 0)
    est_core[core] = jnp.where(row == 0, sums, jnp.where(row == 1, pairs, 0.0))
    core_copy = pltpu.make_async_remote_copy(
        src_ref=est_core.at[core], dst_ref=est_core.at[core], send_sem=c_send, recv_sem=c_recv, device_id=sibling
    )
    core_copy.start()
    core_copy.wait_recv()
    est_all[chip] = est_core[0] + est_core[1]

    def all_copy(delta):
        return pltpu.make_async_remote_copy(
            src_ref=est_all.at[chip], dst_ref=est_all.at[chip], send_sem=a_send.at[delta], recv_sem=a_recv.at[delta],
            device_id=at((chip + delta) % 16),
        )

    def start_all(delta, _):
        all_copy(delta).start()
        return 0

    lax.fori_loop(1, 16, start_all, 0)
    for block in range(TOK // 16):
        at_ = slice(block * 16, (block + 1) * 16)
        normed_ref[at_] = (gain_ref[...] * usum[at_] * inv_root[at_]).astype(bf16)

    for j in range(PLANES):
        end_dispatch(j)
        passed_on(j).wait_send()
        to_sibling(j).wait_send()

        def gone(q, _):
            mine, _, there = give(j, q)

            @pl.when(jnp.logical_not(mine))
            def _():
                there.wait_send()

            return 0

        lax.fori_loop(0, 4, gone, 0)
    for j, unit in UNITS:
        for i in range(3):
            exchange(j, unit, i).wait_send()
    for copy in (early_value(), early_tangent(), late_value(), late_tangent()):
        copy.wait_send()
    for i, who in enumerate((beside, across, diagonal)):
        stat_copy(i, who).wait_send()
    core_copy.wait_send()

    def end_all(delta, _):
        all_copy(delta).wait()
        return 0

    lax.fori_loop(1, 16, end_all, 0)
    mean = jnp.sum(est_all[...], axis=0)
    small_ref[0:2, 0:TOK] = jnp.concatenate(curves, axis=0)
    small_ref[2:3, :] = mean[0:1] / jnp.maximum(mean[1:2], 1.0)


def deliver(normed_in, small_in, normed_ref, curv_ref, est_ref):
    normed_ref[...] = normed_in[...]
    curv_ref[...] = small_in[0:2, 0:TOK]
    est_ref[...] = small_in[2:3, 0:EXPERTS]


def on_device(tokens, targets, norm_gain, expert_ids, gate_prob, w_gate, gate_probe, w_up, w_down):
    vmem = pl.BlockSpec(memory_space=pltpu.VMEM)
    anywhere = pl.BlockSpec(memory_space=pl.ANY)
    dma = pltpu.SemaphoreType.DMA
    normed, small = pl.pallas_call(
        kernel,
        out_shape=(
            jax.ShapeDtypeStruct((TOK, WIDTH), bf16),
            jax.ShapeDtypeStruct((8, 128), f32),
        ),
        in_specs=[vmem] * 5 + [anywhere] * 4,
        out_specs=(vmem, vmem),
        scratch_shapes=[
            pltpu.VMEM((6, WIDTH, HALF), bf16),
            pltpu.VMEM((HIDDEN, WIDTH), bf16),
            pltpu.VMEM((EXPERTS, MAIN, BLOCK), bf16),
            pltpu.VMEM((PLANES, 2, 4, MAIN, BLOCK), bf16),
            pltpu.VMEM((ROWS, WIDTH), bf16),
            pltpu.VMEM((PLANES, 3, ROWS, HIDDEN), bf16),
            pltpu.VMEM((PLANES, 3, ROWS, HIDDEN), bf16),
            pltpu.VMEM((3 * ROWS, HIDDEN), bf16),
            pltpu.VMEM((3, 128, PIECE), bf16),
            pltpu.VMEM((PLANES, 2, 4, 3, MAIN, BLOCK), bf16),
            pltpu.VMEM((PLANES, 4, 3, MAIN, BLOCK), bf16),
            pltpu.VMEM((PLANES, 4, 3, MAIN, BLOCK), bf16),
            pltpu.VMEM((TOK, WIDTH), bf16),
            pltpu.VMEM((TOK, WIDTH), bf16),
            pltpu.VMEM((2, 2 * TOK, WIDTH // 2), f32),
            pltpu.VMEM((2, 2 * TOK, WIDTH // 2), bf16),
            pltpu.VMEM((2 * TOK, WIDTH // 2), bf16),
            pltpu.VMEM((2 * TOK, WIDTH), f32),
            pltpu.VMEM((TOK, WIDTH), f32),
            pltpu.VMEM((2, 2, MAIN, BLOCK), bf16),
            pltpu.VMEM((2, 2, MAIN, WIDTH // 2 + PIECE), bf16),
            pltpu.VMEM((2, MAIN, WIDTH // 2 + PIECE), bf16),
            pltpu.VMEM((4, TOK, 128), f32),
            pltpu.VMEM((2, 8, 128), f32),
            pltpu.VMEM((16, 8, 128), f32),
            dma((7,)),
            dma((PLANES, 4)), dma((PLANES, 4)),
            dma((PLANES,)), dma((PLANES,)),
            dma((PLANES, 3, 3)), dma((PLANES, 3, 3)),
            dma((PLANES,)), dma((PLANES,)),
            dma((PLANES, 4)), dma((PLANES, 4)),
            dma((4,)), dma((4,)),
            dma((3,)), dma((3,)),
            dma, dma,
            dma((16,)), dma((16,)),
        ],
        compiler_params=pltpu.CompilerParams(
            collective_id=0, has_side_effects=True, vmem_limit_bytes=60 * 1024 * 1024
        ),
    )(
        expert_ids.T,
        gate_prob.T,
        norm_gain.reshape(1, WIDTH),
        tokens,
        targets,
        w_gate,
        gate_probe,
        w_up,
        w_down,
    )
    normed, curvature, estimate = pl.pallas_call(
        deliver,
        out_shape=(
            jax.ShapeDtypeStruct((TOK, WIDTH), bf16),
            jax.ShapeDtypeStruct((2, TOK), f32),
            jax.ShapeDtypeStruct((1, EXPERTS), f32),
        ),
        in_specs=[vmem, vmem],
        out_specs=(vmem, vmem, vmem),
    )(normed, small)
    return normed, curvature.T, estimate.reshape(EXPERTS)


def solution(mesh):
    return jax.shard_map(
        on_device,
        mesh=mesh,
        in_specs=(
            P("dp", "tensor"),
            P("dp", "tensor"),
            P("tensor"),
            P("dp", None),
            P("dp", None),
            P("tensor", ("dp", "expert")),
            P("tensor", ("dp", "expert")),
            P("tensor", ("dp", "expert")),
            P(("dp", "expert"), "tensor"),
        ),
        out_specs=(P("dp", "tensor"), P("dp", None), P()),
        check_vma=False,
    )
```

```python
import functools

import jax
import jax.numpy as jnp
from jax import lax
from jax.experimental import pallas as pl
from jax.experimental.pallas import tpu as pltpu
from jax.sharding import PartitionSpec as P

D = 4096
EXPERTS = 8
TOK = 64
CAP = 18
MAIN = 16
FOLD = 8
PLANES = 4
OWNERS = 8
ROWS = OWNERS * CAP
WIDTH = 2048
PIECE = WIDTH // FOLD
BLOCK = WIDTH + PIECE
HIDDEN = 1024
HALF = HIDDEN // 2
OWN = (0, 64)
OTHER = (64, 80)
PART_A = (0, 32)
PART_B = (32, 32)
UNITS = [(0, PART_A), (0, PART_B), (0, OTHER), (1, OTHER), (1, OWN), (2, OTHER), (2, OWN), (3, OTHER), (3, PART_A), (3, PART_B)]
AHEAD = 4


epsilon = 1e-05
loss_weight = 8.0
bf16 = jnp.bfloat16
f32 = jnp.float32


def iota(shape, dim):
    return lax.broadcasted_iota(jnp.int32, shape, dim)


def ones_where(mask):
    return jnp.where(mask, 1.0, 0.0).astype(f32)


def dot(a, b):
    return jnp.dot(a, b, preferred_element_type=f32)


def slot_curvature(inv_root, moments, weighted_uu, resid_b, resid_a, resid_u):
    inv_cube = inv_root * inv_root * inv_root
    first_rate = 2.0 * moments[0] / D
    second_rate = 2.0 * (moments[1] + moments[2]) / D
    slope_one = -0.5 * inv_cube * first_rate
    slope_two = (
        0.75 * inv_cube * inv_root * inv_root * first_rate * first_rate
        - 0.5 * inv_cube * second_rate
    )
    tangent_sq = (
        inv_root * inv_root * moments[3]
        + 2.0 * inv_root * slope_one * moments[4]
        + slope_one * slope_one * weighted_uu
    )
    bending = inv_root * resid_b + 2.0 * slope_one * resid_a + slope_two * resid_u
    return 2.0 * loss_weight / D * (tangent_sq + bending)


def kernel(
    ids_ref, prob_ref, gain_ref, tokens_ref, targets_ref, wg_hbm, wp_hbm, wu_hbm, wd_hbm,
    normed_ref, small_ref,
    w_in, w_down, out_rows, rows, lhs, tsend, trecv, jets, folded, img, sib, ret,
    pown, prec, aown, asend, arec, bown, usum, slot_value, slot_tangent, tangent_out, stat, est_core, est_all,
    w_sem, d_send, d_recv, f_send, f_recv, t_send, t_recv, s_send, s_recv, r_send, r_recv,
    e_send, e_recv, st_send, st_recv, c_send, c_recv, a_send, a_recv,
):
    dp = lax.axis_index("dp")
    x_half = lax.axis_index("expert")
    part = lax.axis_index("tensor")
    z, y, core = dp // 8, (dp // 2) % 4, dp % 2
    chip = dp // 2
    sibling = {"dp": chip * 2 + (1 - core)}
    beside = {"tensor": 1 - part}
    across = {"expert": 1 - x_half}
    diagonal = {"expert": 1 - x_half, "tensor": 1 - part}

    def at(chip_index):
        return {"dp": chip_index * 2 + core}

    barrier = pltpu.get_barrier_semaphore()
    for who in (sibling, beside, across, diagonal):
        pl.semaphore_signal(barrier, inc=1, device_id=who)

    def greet(delta, _):
        pl.semaphore_signal(barrier, inc=1, device_id=at((chip + delta) % 16))
        return 0

    lax.fori_loop(1, 16, greet, 0)

    def weights(i):
        src = (wg_hbm, wp_hbm, wu_hbm)[i // 2].at[:, pl.ds((i % 2) * HALF, HALF)]
        return pltpu.make_async_copy(src, w_in.at[i], w_sem.at[i])

    for i in range(6):
        weights(i).start()
    down = pltpu.make_async_copy(wd_hbm, w_down, w_sem.at[6])
    down.start()

    ids = ids_ref[...]
    names = (ids[0:1, :] == iota((EXPERTS, TOK), 0)) | (ids[1:2, :] == iota((EXPERTS, TOK), 0))
    names = ones_where(names).astype(bf16)
    before = ones_where(iota((TOK, TOK), 0) < iota((TOK, TOK), 1)).astype(bf16)
    count = dot(names, before).astype(bf16)
    spread = ones_where((iota((128, EXPERTS), 0) >> 4) == iota((128, EXPERTS), 1)).astype(bf16)
    slot_of = dot(spread, count).astype(jnp.int32)
    named = dot(spread, names) > 0.5
    line = iota((128, TOK), 0)
    pick_main = ones_where(named & (slot_of == (line & 15))).astype(bf16)
    pick_fold = named & (slot_of == MAIN + (line & 1))
    out_rows[:, :, :WIDTH] = dot(pick_main, tokens_ref[...]).astype(bf16).reshape(EXPERTS, MAIN, WIDTH)
    fold = jnp.zeros((128, PIECE), f32)
    for f in range(FOLD):
        pick = ones_where(pick_fold & (((line >> 1) & 7) == f)).astype(bf16)
        fold = fold + dot(pick, tokens_ref[:, f * PIECE : (f + 1) * PIECE])
    out_rows[:, :, WIDTH:] = fold.astype(bf16).reshape(EXPERTS, MAIN, PIECE)

    pl.semaphore_wait(barrier, 19)

    def plane_of(j, q):
        return (z + (j + 2 * (y // 2) + 2 * (q // 2)) % PLANES) % PLANES

    def dispatch(j, q):
        target = plane_of(j, q) * 4 + q
        block = out_rows.at[plane_of(j, q) * 2 + q // 2]
        here = pltpu.make_async_copy(block, rows.at[j, core, y], d_recv.at[j, y])
        there = pltpu.make_async_remote_copy(
            src_ref=block, dst_ref=rows.at[j, core, y], send_sem=d_send.at[j, q], recv_sem=d_recv.at[j, y],
            device_id=at(target),
        )
        return target == chip, here, there

    def start_dispatch(j):
        def one(q, _):
            mine, here, there = dispatch(j, q)

            @pl.when(mine)
            def _():
                here.start()

            @pl.when(jnp.logical_not(mine))
            def _():
                there.start()

            return 0

        lax.fori_loop(0, 4, one, 0)

    def end_dispatch(j):
        def one(q, _):
            mine, _, there = dispatch(j, q)

            @pl.when(jnp.logical_not(mine))
            def _():
                there.wait_send()

            return 0

        lax.fori_loop(0, 4, one, 0)

    def passed_on(j):
        return pltpu.make_async_remote_copy(
            src_ref=rows.at[j, core], dst_ref=rows.at[j, core], send_sem=f_send.at[j], recv_sem=f_recv.at[j],
            device_id=sibling,
        )

    def owners(j, unit):
        close = 2 * (y // 2)
        away = 2 - close
        if unit not in (PART_A, PART_B):
            return (0, 1, 2, 3)
        if j == 0:
            return (close, close + 1) if unit == PART_A else (away, away + 1)
        return (0, 2) if unit == PART_A else (1, 3)

    def arrived(j, some):
        for q in some:
            pltpu.make_async_copy(out_rows.at[0], rows.at[j, core, q], d_recv.at[j, q]).wait()

    def arrive(j):
        arrived(j, range(4))
        passed_on(j).start()

    a_, b_ = iota((128, 128), 0), iota((128, 128), 1)
    swap = ones_where(
        ((a_ >> 4) == ((b_ >> 1) & 7)) & (((a_ >> 1) & 7) == (b_ >> 4)) & ((a_ & 1) == (b_ & 1))
    ).astype(bf16)

    def exchange(j, unit, i):
        at_ = pl.ds(*unit)
        number = {OWN: 0, OTHER: 1, PART_A: 0, PART_B: 2}[unit]
        return pltpu.make_async_remote_copy(
            src_ref=tsend.at[j, i, at_], dst_ref=trecv.at[j, i, at_],
            send_sem=t_send.at[j, number, i], recv_sem=t_recv.at[j, number, i], device_id=beside,
        )

    def project(j, unit, send):
        first, many = unit
        at_ = slice(first, first + many)
        if unit != OTHER:
            for i, q in enumerate(owners(j, unit)):
                lhs[first + 16 * i : first + 16 * i + 16, :] = rows[j, core, q, :, :WIDTH]
        else:
            passed_on(j).wait_recv()
            lhs[64:128, :] = rows[j, 1 - core, :, :, :WIDTH].reshape(64, WIDTH)
            extra = rows[j, :, :, :, WIDTH:].reshape(128, PIECE)
            extra = dot(swap, extra).astype(bf16)
            for f in range(FOLD):
                lhs[128:, f * PIECE : (f + 1) * PIECE] = extra[f * 16 : (f + 1) * 16]

        def one(i, _):
            for half in range(2):
                w = i * 2 + half
                if j == 0 and unit == PART_A:
                    pltpu.make_async_copy(w_in.at[w], w_in.at[w], w_sem.at[w]).wait()
                tsend[j, i, at_, half * HALF : (half + 1) * HALF] = dot(lhs[at_, :], w_in[w]).astype(bf16)
            if send:
                exchange(j, unit, i).start()
            return 0

        lax.fori_loop(0, 3, one, 0)

    def to_sibling(j):
        return pltpu.make_async_remote_copy(
            src_ref=img.at[j, 1 - core], dst_ref=sib.at[j], send_sem=s_send.at[j], recv_sem=s_recv.at[j],
            device_id=sibling,
        )

    def expand(j, unit, following, then=None):
        first, many = unit
        for i in range(3):
            exchange(j, unit, i).wait_recv()
        if following:
            for i in range(3):
                exchange(*following, i).start()
        if then:
            then()

        def one(block, _):
            at_ = pl.ds(pl.multiple_of(first + block * 16, 16), 16)

            def pre(i):
                return tsend[j, i, at_].astype(f32) + trecv[j, i, at_].astype(f32)

            g, d, u = pre(0), pre(1), pre(2)
            s = jax.nn.sigmoid(g)
            slope = s * (1.0 + g * (1.0 - s))
            second = s * (1.0 - s) * (2.0 + g * (1.0 - 2.0 * s))
            jets[pl.ds(pl.multiple_of(block * 16, 16), 16)] = (g * s * u).astype(bf16)
            jets[pl.ds(pl.multiple_of(many + block * 16, 16), 16)] = (slope * d * u).astype(bf16)
            jets[pl.ds(pl.multiple_of(2 * many + block * 16, 16), 16)] = (second * d * d * u).astype(bf16)
            return 0

        lax.fori_loop(0, many // 16, one, 0)
        if j == 0 and unit == PART_A:
            down.wait()
        whose = 1 - core if unit == OTHER else core

        def piece(n, _):
            cols = pl.ds(pl.multiple_of(n * PIECE, PIECE), PIECE)
            out = dot(jets[: 3 * many], w_down[:, cols]).astype(bf16)
            for i in range(3):
                top = i * many
                for n_, q in enumerate(owners(j, unit)):
                    img[j, whose, q, i, :, cols] = out[top + 16 * n_ : top + 16 * n_ + 16]
                if unit == OTHER:
                    folded[i, pl.ds(pl.multiple_of(n * 16, 16), 16)] = out[top + 64 : top + 80]
            return 0

        lax.fori_loop(0, FOLD, piece, 0)
        if unit == OTHER:
            for i in range(3):
                extra = dot(swap, folded[i]).astype(bf16)
                img[j, :, :, i, :, WIDTH:] = extra.reshape(2, 4, MAIN, PIECE)
            to_sibling(j).start()

    def give(j, q):
        target = ((z + PLANES - (j + 2 * (q // 2) + 2 * (y // 2)) % PLANES) % PLANES) * 4 + q
        here = pltpu.make_async_copy(img.at[j, core, q], ret.at[j, y], r_recv.at[j, y])
        there = pltpu.make_async_remote_copy(
            src_ref=img.at[j, core, q], dst_ref=ret.at[j, y], send_sem=r_send.at[j, q], recv_sem=r_recv.at[j, y],
            device_id=at(target),
        )
        return target == chip, here, there

    def give_back(j, some=(0, 1, 2, 3), first=True):
        if first:
            to_sibling(j).wait_recv()

        def one(q):
            img[j, core, q] = (img[j, core, q].astype(f32) + sib[j, q].astype(f32)).astype(bf16)
            mine, here, there = give(j, q)

            @pl.when(mine)
            def _():
                here.start()

            @pl.when(jnp.logical_not(mine))
            def _():
                there.start()

        for q in some:
            one(q)

    eye_tok = iota((TOK, TOK), 0) == iota((TOK, TOK), 1)

    def upright(row):
        return jnp.sum(jnp.where(eye_tok, row, 0.0), axis=1, keepdims=True)

    prob_col = jnp.concatenate([upright(prob_ref[k : k + 1, :]) for k in range(2)], axis=0)
    id_col = [upright(ids[k : k + 1, :].astype(f32)) for k in range(2)]

    def back(many, place):
        line = iota((many, TOK), 0)

        def expert(line):
            j, pair = place(line)
            return ((z + ((j + 2 * (y // 2) + 2 * pair) & 3)) & 3) * 2 + pair

        spread = ones_where(expert(iota((many, EXPERTS), 0)) == iota((many, EXPERTS), 1)).astype(bf16)
        slot = dot(spread, count).astype(jnp.int32)

        def for_ids(wanted):
            masks = [(expert(line) == ids[k : k + 1, :]) & (slot == wanted) for k in range(2)]
            return jnp.concatenate([ones_where(m).T for m in masks], axis=0)

        return for_ids(line & 15).astype(bf16), for_ids(MAIN + (line & 1)), (iota((2 * TOK, many), 1) >> 1) & 7

    def picked(backs, whole, extra, f):
        main, fold, index = backs
        pick = jnp.where(index == f, fold, 0.0).astype(bf16)
        return prob_col * (dot(main, whole) + dot(pick, extra))

    def across_copy(i, src, dst):
        return pltpu.make_async_remote_copy(
            src_ref=src, dst_ref=dst, send_sem=e_send.at[i], recv_sem=e_recv.at[i], device_id=across
        )

    def early_value():
        return across_copy(0, pown, prec)

    def early_tangent():
        return across_copy(1, asend.at[1 - x_half], arec)

    def late_value():
        return across_copy(2, slot_value.at[x_half], slot_value.at[x_half])

    def late_tangent():
        return across_copy(3, tangent_out, slot_tangent.at[x_half])

    def returned(j):
        for q in range(4):
            pltpu.make_async_copy(ret.at[j, q], ret.at[j, q], r_recv.at[j, q]).wait()

    def early():
        backs = back(64 * (PLANES - 1), lambda line: (line >> 6, (line >> 5) & 1))
        for j in range(PLANES - 1):
            returned(j)

        def piece(f, _):
            cols = pl.ds(pl.multiple_of(f * PIECE, PIECE), PIECE)
            half_cols = pl.ds(pl.multiple_of((f % 4) * PIECE, PIECE), PIECE)

            def of(i):
                whole = ret[: PLANES - 1, :, i, :, cols].reshape(64 * (PLANES - 1), PIECE)
                extra = ret[: PLANES - 1, :, i, :, WIDTH:].reshape(64 * (PLANES - 1), PIECE)
                return picked(backs, whole, extra, f)

            value = of(0)
            pown[:, cols] = (value[:TOK] + value[TOK:]).astype(bf16)
            tangent = of(1)
            aown[f // 4, :, half_cols] = tangent
            asend[f // 4, :, half_cols] = tangent.astype(bf16)
            bown[:, cols] = of(2)
            return 0

        lax.fori_loop(0, FOLD, piece, 0)

    def send_early():
        early_value().start()
        early_tangent().start()

    start_dispatch(0)
    arrived(0, owners(0, PART_A))
    project(*UNITS[0], True)
    arrived(0, owners(0, PART_B))
    passed_on(0).start()
    start_dispatch(1)
    project(*UNITS[1], True)
    project(*UNITS[2], True)
    arrive(1)
    start_dispatch(2)
    start_dispatch(3)
    project(*UNITS[3], True)
    for n, (j, unit) in enumerate(UNITS):
        last = n == len(UNITS) - 1
        expand(j, unit, UNITS[n + 2] if AHEAD <= n + 2 < len(UNITS) else None, send_early if last else None)
        if n < 2:
            arrive(n + 2)
        if n + 4 < len(UNITS):
            project(*UNITS[n + 4], False)
        if n == 3:
            give_back(0)
        if unit == OWN:
            give_back(j)
        if j == 3 and unit != OTHER:
            give_back(j, owners(j, unit), unit == PART_A)
        if (j, unit) == (3, OTHER):
            early()

    final = PLANES - 1
    near = pl.ds(pl.multiple_of(x_half * (WIDTH // 2), WIDTH // 2), WIDTH // 2)
    far = pl.ds(pl.multiple_of((1 - x_half) * (WIDTH // 2), WIDTH // 2), WIDTH // 2)
    late_backs = back(64, lambda line: (final, (line >> 4) & 1))
    second_backs = back(64, lambda line: (final, (line >> 5) & 1))
    returned(final)

    def pair_sum(pair, i, cols):
        both = ret[final, 2 * pair, i, :, cols].astype(f32) + ret[final, 2 * pair + 1, i, :, cols].astype(f32)
        return both.astype(bf16)

    for pair in range(2):
        slot_value[x_half, pair] = pair_sum(pair, 0, slice(0, BLOCK))
    late_value().start()
    for pair in range(2):
        tangent_out[pair, :, : WIDTH // 2] = pair_sum(pair, 1, far)
        tangent_out[pair, :, WIDTH // 2 :] = pair_sum(pair, 1, slice(WIDTH, BLOCK))
    late_tangent().start()
    for pair in range(2):
        slot_tangent[x_half, pair, :, : WIDTH // 2] = pair_sum(pair, 1, near)
        slot_tangent[x_half, pair, :, WIDTH // 2 :] = pair_sum(pair, 1, slice(WIDTH, BLOCK))

    def late_second(f, _):
        cols = pl.ds(pl.multiple_of(f * PIECE, PIECE), PIECE)
        whole = ret[final, :, 2, :, cols].reshape(64, PIECE)
        extra = ret[final, :, 2, :, WIDTH:].reshape(64, PIECE)
        bown[:, cols] += picked(second_backs, whole, extra, f)
        return 0

    lax.fori_loop(0, FOLD, late_second, 0)

    def late_piece(f, _):
        cols = pl.ds(pl.multiple_of(f * PIECE, PIECE), PIECE)
        whole = slot_value[:, :, :, cols].reshape(64, PIECE)
        extra = slot_value[:, :, :, WIDTH:].reshape(64, PIECE)
        value = picked(late_backs, whole, extra, f)
        usum[:, cols] = value[:TOK] + value[TOK:]
        return 0

    def late_slope(f, _):
        cols = pl.ds(pl.multiple_of(f * PIECE, PIECE), PIECE)
        whole = slot_tangent[:, :, :, cols].reshape(64, PIECE)
        extra = slot_tangent[:, :, :, WIDTH // 2 :].reshape(64, PIECE)
        aown[x_half, :, cols] += picked(late_backs, whole, extra, x_half * 4 + f)
        return 0

    me = x_half * 2 + part
    lane = iota((16, 128), 1)

    def over(v):
        return jnp.sum(v, axis=-1, keepdims=True)

    def lay(values, laid):
        for i, value in values.items():
            laid = jnp.where(lane == i, value, laid)
        return laid

    def inner_value(block, _):
        at_ = pl.ds(pl.multiple_of(block * 16, 16), 16)
        u = tokens_ref[at_].astype(f32) + (pown[at_].astype(f32) + prec[at_].astype(f32)) + usum[at_]
        usum[at_] = u
        gain = gain_ref[...]
        heavy = gain * gain * u
        goal = gain * targets_ref[at_].astype(f32)
        stats = {}
        for k in range(2):
            b = bown[pl.ds(pl.multiple_of(k * TOK + block * 16, 16), 16)]
            stats[3 + k * 8 + 2] = over(u * b)
            stats[3 + k * 8 + 5] = over(heavy * b)
            stats[3 + k * 8 + 6] = over(goal * b)
        gain = gain_ref[:, near]
        u = usum[at_, near]
        heavy = gain * gain * u
        goal = gain * targets_ref[at_, near].astype(f32)
        stats[0] = over(u * u)
        stats[1] = over(heavy * u)
        stats[2] = over(goal * u)
        stat[me, at_] = lay(stats, jnp.zeros((16, 128), f32))
        return 0

    def inner_tangent(block, _):
        at_ = pl.ds(pl.multiple_of(block * 16, 16), 16)
        gain = gain_ref[:, near]
        u = usum[at_, near]
        heavy = gain * gain * u
        goal = gain * targets_ref[at_, near].astype(f32)
        stats = {}
        for k in range(2):
            own = pl.ds(pl.multiple_of(k * TOK + block * 16, 16), 16)
            a = aown[x_half, own] + arec[own].astype(f32)
            stats[3 + k * 8 + 0] = over(u * a)
            stats[3 + k * 8 + 1] = over(a * a)
            stats[3 + k * 8 + 3] = over(gain * gain * a * a)
            stats[3 + k * 8 + 4] = over(heavy * a)
            stats[3 + k * 8 + 7] = over(goal * a)
        stat[me, at_] = lay(stats, stat[me, at_])
        return 0

    early_value().wait_recv()
    late_value().wait_recv()
    lax.fori_loop(0, FOLD, late_piece, 0)
    lax.fori_loop(0, TOK // 16, inner_value, 0)
    early_tangent().wait_recv()
    late_tangent().wait_recv()
    lax.fori_loop(0, FOLD // 2, late_slope, 0)
    lax.fori_loop(0, TOK // 16, inner_tangent, 0)

    def stat_copy(i, who):
        return pltpu.make_async_remote_copy(
            src_ref=stat.at[me], dst_ref=stat.at[me], send_sem=st_send.at[i], recv_sem=st_recv.at[i], device_id=who
        )

    for i, who in enumerate((beside, across, diagonal)):
        stat_copy(i, who).start()
    for i, who in enumerate((beside, across, diagonal)):
        stat_copy(i, who).wait_recv()
    total = (stat[0] + stat[1]) + (stat[2] + stat[3])

    def column(i):
        return total[:, i : i + 1]

    inv_root = lax.rsqrt(column(0) / D + epsilon)
    weighted_uu = column(1)
    resid_u = inv_root * weighted_uu - column(2)
    sums = jnp.zeros((1, 128), f32)
    pairs = jnp.zeros((1, 128), f32)
    curves = []
    for k in range(2):
        m = [column(3 + k * 8 + i) for i in range(8)]
        curve = slot_curvature(
            inv_root, m[:5], weighted_uu, inv_root * m[5] - m[6], inv_root * m[4] - m[7], resid_u
        )
        curves.append(jnp.sum(jnp.where(eye_tok, curve, 0.0), axis=0, keepdims=True))
        member = ones_where(iota((TOK, 128), 1).astype(f32) == id_col[k])
        sums = sums + jnp.sum(member * curve, axis=0, keepdims=True)
        pairs = pairs + jnp.sum(member, axis=0, keepdims=True)
    row = iota((8, 128), 0)
    est_core[core] = jnp.where(row == 0, sums, jnp.where(row == 1, pairs, 0.0))
    core_copy = pltpu.make_async_remote_copy(
        src_ref=est_core.at[core], dst_ref=est_core.at[core], send_sem=c_send, recv_sem=c_recv, device_id=sibling
    )
    core_copy.start()
    core_copy.wait_recv()
    est_all[chip] = est_core[0] + est_core[1]

    def all_copy(delta):
        return pltpu.make_async_remote_copy(
            src_ref=est_all.at[chip], dst_ref=est_all.at[chip], send_sem=a_send.at[delta], recv_sem=a_recv.at[delta],
            device_id=at((chip + delta) % 16),
        )

    def start_all(delta, _):
        all_copy(delta).start()
        return 0

    lax.fori_loop(1, 16, start_all, 0)
    for block in range(TOK // 16):
        at_ = slice(block * 16, (block + 1) * 16)
        normed_ref[at_] = (gain_ref[...] * usum[at_] * inv_root[at_]).astype(bf16)

    for j in range(PLANES):
        end_dispatch(j)
        passed_on(j).wait_send()
        to_sibling(j).wait_send()

        def gone(q, _):
            mine, _, there = give(j, q)

            @pl.when(jnp.logical_not(mine))
            def _():
                there.wait_send()

            return 0

        lax.fori_loop(0, 4, gone, 0)
    for j, unit in UNITS:
        for i in range(3):
            exchange(j, unit, i).wait_send()
    for copy in (early_value(), early_tangent(), late_value(), late_tangent()):
        copy.wait_send()
    for i, who in enumerate((beside, across, diagonal)):
        stat_copy(i, who).wait_send()
    core_copy.wait_send()

    def end_all(delta, _):
        all_copy(delta).wait()
        return 0

    lax.fori_loop(1, 16, end_all, 0)
    mean = jnp.sum(est_all[...], axis=0)
    small_ref[0:2, 0:TOK] = jnp.concatenate(curves, axis=0)
    small_ref[2:3, :] = mean[0:1] / jnp.maximum(mean[1:2], 1.0)


def deliver(normed_in, small_in, normed_ref, curv_ref, est_ref):
    normed_ref[...] = normed_in[...]
    curv_ref[...] = small_in[0:2, 0:TOK]
    est_ref[...] = small_in[2:3, 0:EXPERTS]


def on_device(tokens, targets, norm_gain, expert_ids, gate_prob, w_gate, gate_probe, w_up, w_down):
    vmem = pl.BlockSpec(memory_space=pltpu.VMEM)
    anywhere = pl.BlockSpec(memory_space=pl.ANY)
    dma = pltpu.SemaphoreType.DMA
    normed, small = pl.pallas_call(
        kernel,
        out_shape=(
            jax.ShapeDtypeStruct((TOK, WIDTH), bf16),
            jax.ShapeDtypeStruct((8, 128), f32),
        ),
        in_specs=[vmem] * 5 + [anywhere] * 4,
        out_specs=(vmem, vmem),
        scratch_shapes=[
            pltpu.VMEM((6, WIDTH, HALF), bf16),
            pltpu.VMEM((HIDDEN, WIDTH), bf16),
            pltpu.VMEM((EXPERTS, MAIN, BLOCK), bf16),
            pltpu.VMEM((PLANES, 2, 4, MAIN, BLOCK), bf16),
            pltpu.VMEM((ROWS, WIDTH), bf16),
            pltpu.VMEM((PLANES, 3, ROWS, HIDDEN), bf16),
            pltpu.VMEM((PLANES, 3, ROWS, HIDDEN), bf16),
            pltpu.VMEM((3 * ROWS, HIDDEN), bf16),
            pltpu.VMEM((3, 128, PIECE), bf16),
            pltpu.VMEM((PLANES, 2, 4, 3, MAIN, BLOCK), bf16),
            pltpu.VMEM((PLANES, 4, 3, MAIN, BLOCK), bf16),
            pltpu.VMEM((PLANES, 4, 3, MAIN, BLOCK), bf16),
            pltpu.VMEM((TOK, WIDTH), bf16),
            pltpu.VMEM((TOK, WIDTH), bf16),
            pltpu.VMEM((2, 2 * TOK, WIDTH // 2), f32),
            pltpu.VMEM((2, 2 * TOK, WIDTH // 2), bf16),
            pltpu.VMEM((2 * TOK, WIDTH // 2), bf16),
            pltpu.VMEM((2 * TOK, WIDTH), f32),
            pltpu.VMEM((TOK, WIDTH), f32),
            pltpu.VMEM((2, 2, MAIN, BLOCK), bf16),
            pltpu.VMEM((2, 2, MAIN, WIDTH // 2 + PIECE), bf16),
            pltpu.VMEM((2, MAIN, WIDTH // 2 + PIECE), bf16),
            pltpu.VMEM((4, TOK, 128), f32),
            pltpu.VMEM((2, 8, 128), f32),
            pltpu.VMEM((16, 8, 128), f32),
            dma((7,)),
            dma((PLANES, 4)), dma((PLANES, 4)),
            dma((PLANES,)), dma((PLANES,)),
            dma((PLANES, 3, 3)), dma((PLANES, 3, 3)),
            dma((PLANES,)), dma((PLANES,)),
            dma((PLANES, 4)), dma((PLANES, 4)),
            dma((4,)), dma((4,)),
            dma((3,)), dma((3,)),
            dma, dma,
            dma((16,)), dma((16,)),
        ],
        compiler_params=pltpu.CompilerParams(
            collective_id=0, has_side_effects=True, vmem_limit_bytes=60 * 1024 * 1024
        ),
    )(
        expert_ids.T,
        gate_prob.T,
        norm_gain.reshape(1, WIDTH),
        tokens,
        targets,
        w_gate,
        gate_probe,
        w_up,
        w_down,
    )
    normed, curvature, estimate = pl.pallas_call(
        deliver,
        out_shape=(
            jax.ShapeDtypeStruct((TOK, WIDTH), bf16),
            jax.ShapeDtypeStruct((2, TOK), f32),
            jax.ShapeDtypeStruct((1, EXPERTS), f32),
        ),
        in_specs=[vmem, vmem],
        out_specs=(vmem, vmem, vmem),
    )(normed, small)
    return normed, curvature.T, estimate.reshape(EXPERTS)


def solution(mesh):
    return jax.shard_map(
        on_device,
        mesh=mesh,
        in_specs=(
            P("dp", "tensor"),
            P("dp", "tensor"),
            P("tensor"),
            P("dp", None),
            P("dp", None),
            P("tensor", ("dp", "expert")),
            P("tensor", ("dp", "expert")),
            P("tensor", ("dp", "expert")),
            P(("dp", "expert"), "tensor"),
        ),
        out_specs=(P("dp", "tensor"), P("dp", None), P()),
        check_vma=False,
    )
```

```python
import functools

import jax
import jax.numpy as jnp
from jax import lax
from jax.experimental import pallas as pl
from jax.experimental.pallas import tpu as pltpu
from jax.sharding import PartitionSpec as P

D = 4096
EXPERTS = 8
TOK = 64
CAP = 18
MAIN = 16
FOLD = 8
PLANES = 4
OWNERS = 8
ROWS = OWNERS * CAP
WIDTH = 2048
PIECE = WIDTH // FOLD
BLOCK = WIDTH + PIECE
HIDDEN = 1024
HALF = HIDDEN // 2
OWN = (0, 64)
OTHER = (64, 80)
PART_A = (0, 32)
PART_B = (32, 32)
UNITS = [(0, PART_A), (0, PART_B), (0, OTHER), (1, OTHER), (1, OWN), (2, OTHER), (2, OWN), (3, OTHER), (3, PART_A), (3, PART_B)]
AHEAD = 4


epsilon = 1e-05
loss_weight = 8.0
bf16 = jnp.bfloat16
f32 = jnp.float32


def iota(shape, dim):
    return lax.broadcasted_iota(jnp.int32, shape, dim)


def ones_where(mask):
    return jnp.where(mask, 1.0, 0.0).astype(f32)


def dot(a, b):
    return jnp.dot(a, b, preferred_element_type=f32)


def slot_curvature(inv_root, moments, weighted_uu, resid_b, resid_a, resid_u):
    inv_cube = inv_root * inv_root * inv_root
    first_rate = 2.0 * moments[0] / D
    second_rate = 2.0 * (moments[1] + moments[2]) / D
    slope_one = -0.5 * inv_cube * first_rate
    slope_two = (
        0.75 * inv_cube * inv_root * inv_root * first_rate * first_rate
        - 0.5 * inv_cube * second_rate
    )
    tangent_sq = (
        inv_root * inv_root * moments[3]
        + 2.0 * inv_root * slope_one * moments[4]
        + slope_one * slope_one * weighted_uu
    )
    bending = inv_root * resid_b + 2.0 * slope_one * resid_a + slope_two * resid_u
    return 2.0 * loss_weight / D * (tangent_sq + bending)


def kernel(
    ids_ref, prob_ref, gain_ref, tokens_ref, targets_ref, wg_hbm, wp_hbm, wu_hbm, wd_hbm,
    normed_ref, small_ref,
    w_in, w_down, out_rows, rows, lhs, tsend, trecv, jets, folded, img, sib, ret,
    pown, prec, aown, asend, arec, bown, usum, slot_value, slot_tangent, tangent_out, stat, est_core, est_all,
    w_sem, d_send, d_recv, f_send, f_recv, t_send, t_recv, s_send, s_recv, r_send, r_recv,
    e_send, e_recv, st_send, st_recv, c_send, c_recv, a_send, a_recv,
):
    dp = lax.axis_index("dp")
    x_half = lax.axis_index("expert")
    part = lax.axis_index("tensor")
    z, y, core = dp // 8, (dp // 2) % 4, dp % 2
    chip = dp // 2
    sibling = {"dp": chip * 2 + (1 - core)}
    beside = {"tensor": 1 - part}
    across = {"expert": 1 - x_half}
    diagonal = {"expert": 1 - x_half, "tensor": 1 - part}

    def at(chip_index):
        return {"dp": chip_index * 2 + core}

    barrier = pltpu.get_barrier_semaphore()
    for who in (sibling, beside, across, diagonal):
        pl.semaphore_signal(barrier, inc=1, device_id=who)

    def greet(delta, _):
        pl.semaphore_signal(barrier, inc=1, device_id=at((chip + delta) % 16))
        return 0

    lax.fori_loop(1, 16, greet, 0)

    def weights(i):
        src = (wg_hbm, wp_hbm, wu_hbm)[i // 2].at[:, pl.ds((i % 2) * HALF, HALF)]
        return pltpu.make_async_copy(src, w_in.at[i], w_sem.at[i])

    for i in range(6):
        weights(i).start()
    down = pltpu.make_async_copy(wd_hbm, w_down, w_sem.at[6])
    down.start()

    ids = ids_ref[...]
    names = (ids[0:1, :] == iota((EXPERTS, TOK), 0)) | (ids[1:2, :] == iota((EXPERTS, TOK), 0))
    names = ones_where(names).astype(bf16)
    before = ones_where(iota((TOK, TOK), 0) < iota((TOK, TOK), 1)).astype(bf16)
    count = dot(names, before).astype(bf16)
    spread = ones_where((iota((128, EXPERTS), 0) >> 4) == iota((128, EXPERTS), 1)).astype(bf16)
    slot_of = dot(spread, count).astype(jnp.int32)
    named = dot(spread, names) > 0.5
    line = iota((128, TOK), 0)
    pick_main = ones_where(named & (slot_of == (line & 15))).astype(bf16)
    pick_fold = named & (slot_of == MAIN + (line & 1))
    out_rows[:, :, :WIDTH] = dot(pick_main, tokens_ref[...]).astype(bf16).reshape(EXPERTS, MAIN, WIDTH)
    fold = jnp.zeros((128, PIECE), f32)
    for f in range(FOLD):
        pick = ones_where(pick_fold & (((line >> 1) & 7) == f)).astype(bf16)
        fold = fold + dot(pick, tokens_ref[:, f * PIECE : (f + 1) * PIECE])
    out_rows[:, :, WIDTH:] = fold.astype(bf16).reshape(EXPERTS, MAIN, PIECE)

    pl.semaphore_wait(barrier, 19)

    def plane_of(j, q):
        return (z + (j + 2 * (y // 2) + 2 * (q // 2)) % PLANES) % PLANES

    def dispatch(j, q):
        target = plane_of(j, q) * 4 + q
        block = out_rows.at[plane_of(j, q) * 2 + q // 2]
        here = pltpu.make_async_copy(block, rows.at[j, core, y], d_recv.at[j, y])
        there = pltpu.make_async_remote_copy(
            src_ref=block, dst_ref=rows.at[j, core, y], send_sem=d_send.at[j, q], recv_sem=d_recv.at[j, y],
            device_id=at(target),
        )
        return target == chip, here, there

    def start_dispatch(j):
        def one(q, _):
            mine, here, there = dispatch(j, q)

            @pl.when(mine)
            def _():
                here.start()

            @pl.when(jnp.logical_not(mine))
            def _():
                there.start()

            return 0

        lax.fori_loop(0, 4, one, 0)

    def end_dispatch(j):
        def one(q, _):
            mine, _, there = dispatch(j, q)

            @pl.when(jnp.logical_not(mine))
            def _():
                there.wait_send()

            return 0

        lax.fori_loop(0, 4, one, 0)

    def passed_on(j):
        return pltpu.make_async_remote_copy(
            src_ref=rows.at[j, core], dst_ref=rows.at[j, core], send_sem=f_send.at[j], recv_sem=f_recv.at[j],
            device_id=sibling,
        )

    def owners(j, unit):
        close = 2 * (y // 2)
        away = 2 - close
        if unit not in (PART_A, PART_B):
            return (0, 1, 2, 3)
        if j == 0:
            return (close, close + 1) if unit == PART_A else (away, away + 1)
        return (0, 2) if unit == PART_A else (1, 3)

    def arrived(j, some):
        for q in some:
            pltpu.make_async_copy(out_rows.at[0], rows.at[j, core, q], d_recv.at[j, q]).wait()

    def arrive(j):
        arrived(j, range(4))
        passed_on(j).start()

    a_, b_ = iota((128, 128), 0), iota((128, 128), 1)
    swap = ones_where(
        ((a_ >> 4) == ((b_ >> 1) & 7)) & (((a_ >> 1) & 7) == (b_ >> 4)) & ((a_ & 1) == (b_ & 1))
    ).astype(bf16)

    def exchange(j, unit, i):
        at_ = pl.ds(*unit)
        number = {OWN: 0, OTHER: 1, PART_A: 0, PART_B: 2}[unit]
        return pltpu.make_async_remote_copy(
            src_ref=tsend.at[j, i, at_], dst_ref=trecv.at[j, i, at_],
            send_sem=t_send.at[j, number, i], recv_sem=t_recv.at[j, number, i], device_id=beside,
        )

    def project(j, unit, send):
        first, many = unit
        at_ = slice(first, first + many)
        if unit != OTHER:
            for i, q in enumerate(owners(j, unit)):
                lhs[first + 16 * i : first + 16 * i + 16, :] = rows[j, core, q, :, :WIDTH]
        else:
            passed_on(j).wait_recv()
            lhs[64:128, :] = rows[j, 1 - core, :, :, :WIDTH].reshape(64, WIDTH)
            extra = rows[j, :, :, :, WIDTH:].reshape(128, PIECE)
            extra = dot(swap, extra).astype(bf16)
            for f in range(FOLD):
                lhs[128:, f * PIECE : (f + 1) * PIECE] = extra[f * 16 : (f + 1) * 16]

        def one(i, _):
            for half in range(2):
                w = i * 2 + half
                if j == 0 and unit == PART_A:
                    pltpu.make_async_copy(w_in.at[w], w_in.at[w], w_sem.at[w]).wait()
                tsend[j, i, at_, half * HALF : (half + 1) * HALF] = dot(lhs[at_, :], w_in[w]).astype(bf16)
            if send:
                exchange(j, unit, i).start()
            return 0

        lax.fori_loop(0, 3, one, 0)

    def to_sibling(j):
        return pltpu.make_async_remote_copy(
            src_ref=img.at[j, 1 - core], dst_ref=sib.at[j], send_sem=s_send.at[j], recv_sem=s_recv.at[j],
            device_id=sibling,
        )

    def expand(j, unit, following, then=None):
        first, many = unit
        for i in range(3):
            exchange(j, unit, i).wait_recv()
        if following:
            for i in range(3):
                exchange(*following, i).start()
        if then:
            then()

        def one(block, _):
            at_ = pl.ds(pl.multiple_of(first + block * 16, 16), 16)

            def pre(i):
                return tsend[j, i, at_].astype(f32) + trecv[j, i, at_].astype(f32)

            g, d, u = pre(0), pre(1), pre(2)
            s = jax.nn.sigmoid(g)
            slope = s * (1.0 + g * (1.0 - s))
            second = s * (1.0 - s) * (2.0 + g * (1.0 - 2.0 * s))
            jets[pl.ds(pl.multiple_of(block * 16, 16), 16)] = (g * s * u).astype(bf16)
            jets[pl.ds(pl.multiple_of(many + block * 16, 16), 16)] = (slope * d * u).astype(bf16)
            jets[pl.ds(pl.multiple_of(2 * many + block * 16, 16), 16)] = (second * d * d * u).astype(bf16)
            return 0

        lax.fori_loop(0, many // 16, one, 0)
        if j == 0 and unit == PART_A:
            down.wait()
        whose = 1 - core if unit == OTHER else core

        def piece(n, _):
            cols = pl.ds(pl.multiple_of(n * PIECE, PIECE), PIECE)
            out = dot(jets[: 3 * many], w_down[:, cols]).astype(bf16)
            for i in range(3):
                top = i * many
                for n_, q in enumerate(owners(j, unit)):
                    img[j, whose, q, i, :, cols] = out[top + 16 * n_ : top + 16 * n_ + 16]
                if unit == OTHER:
                    folded[i, pl.ds(pl.multiple_of(n * 16, 16), 16)] = out[top + 64 : top + 80]
            return 0

        lax.fori_loop(0, FOLD, piece, 0)
        if unit == OTHER:
            for i in range(3):
                extra = dot(swap, folded[i]).astype(bf16)
                img[j, :, :, i, :, WIDTH:] = extra.reshape(2, 4, MAIN, PIECE)
            to_sibling(j).start()

    def cuts(j):
        return ((j, 0, 3),) if j < PLANES - 1 else ((j, 0, 2), (j + 1, 2, 1))

    def give(j, q, cut):
        number, low, many = cut
        target = ((z + PLANES - (j + 2 * (q // 2) + 2 * (y // 2)) % PLANES) % PLANES) * 4 + q
        src, dst = img.at[j, core, q, pl.ds(low, many)], ret.at[j, y, pl.ds(low, many)]
        here = pltpu.make_async_copy(src, dst, r_recv.at[number, y])
        there = pltpu.make_async_remote_copy(
            src_ref=src, dst_ref=dst, send_sem=r_send.at[number, q], recv_sem=r_recv.at[number, y], device_id=at(target)
        )
        return target == chip, here, there

    def give_back(j, some=(0, 1, 2, 3), first=True):
        if first:
            to_sibling(j).wait_recv()

        def one(q, cut):
            _, low, many = cut
            own = slice(low, low + many)
            img[j, core, q, own] = (img[j, core, q, own].astype(f32) + sib[j, q, own].astype(f32)).astype(bf16)
            mine, here, there = give(j, q, cut)

            @pl.when(mine)
            def _():
                here.start()

            @pl.when(jnp.logical_not(mine))
            def _():
                there.start()

        for cut in cuts(j):
            for q in some:
                one(q, cut)

    eye_tok = iota((TOK, TOK), 0) == iota((TOK, TOK), 1)

    def upright(row):
        return jnp.sum(jnp.where(eye_tok, row, 0.0), axis=1, keepdims=True)

    prob_col = jnp.concatenate([upright(prob_ref[k : k + 1, :]) for k in range(2)], axis=0)
    id_col = [upright(ids[k : k + 1, :].astype(f32)) for k in range(2)]

    def back(many, place):
        line = iota((many, TOK), 0)

        def expert(line):
            j, pair = place(line)
            return ((z + ((j + 2 * (y // 2) + 2 * pair) & 3)) & 3) * 2 + pair

        spread = ones_where(expert(iota((many, EXPERTS), 0)) == iota((many, EXPERTS), 1)).astype(bf16)
        slot = dot(spread, count).astype(jnp.int32)

        def for_ids(wanted):
            masks = [(expert(line) == ids[k : k + 1, :]) & (slot == wanted) for k in range(2)]
            return jnp.concatenate([ones_where(m).T for m in masks], axis=0)

        return for_ids(line & 15).astype(bf16), for_ids(MAIN + (line & 1)), (iota((2 * TOK, many), 1) >> 1) & 7

    def picked(backs, whole, extra, f):
        main, fold, index = backs
        pick = jnp.where(index == f, fold, 0.0).astype(bf16)
        return prob_col * (dot(main, whole) + dot(pick, extra))

    def across_copy(i, src, dst):
        return pltpu.make_async_remote_copy(
            src_ref=src, dst_ref=dst, send_sem=e_send.at[i], recv_sem=e_recv.at[i], device_id=across
        )

    def early_value():
        return across_copy(0, pown, prec)

    def early_tangent():
        return across_copy(1, asend.at[1 - x_half], arec)

    def late_value():
        return across_copy(2, slot_value.at[x_half], slot_value.at[x_half])

    def late_tangent():
        return across_copy(3, tangent_out, slot_tangent.at[x_half])

    def returned(j, cut):
        number, low, many = cut
        for q in range(4):
            block = ret.at[j, q, pl.ds(low, many)]
            pltpu.make_async_copy(block, block, r_recv.at[number, q]).wait()

    def early():
        backs = back(64 * (PLANES - 1), lambda line: (line >> 6, (line >> 5) & 1))
        for j in range(PLANES - 1):
            returned(j, cuts(j)[0])

        def piece(f, _):
            cols = pl.ds(pl.multiple_of(f * PIECE, PIECE), PIECE)
            half_cols = pl.ds(pl.multiple_of((f % 4) * PIECE, PIECE), PIECE)

            def of(i):
                whole = ret[: PLANES - 1, :, i, :, cols].reshape(64 * (PLANES - 1), PIECE)
                extra = ret[: PLANES - 1, :, i, :, WIDTH:].reshape(64 * (PLANES - 1), PIECE)
                return picked(backs, whole, extra, f)

            value = of(0)
            pown[:, cols] = (value[:TOK] + value[TOK:]).astype(bf16)
            tangent = of(1)
            aown[f // 4, :, half_cols] = tangent
            asend[f // 4, :, half_cols] = tangent.astype(bf16)
            bown[:, cols] = of(2)
            return 0

        lax.fori_loop(0, FOLD, piece, 0)

    def send_early():
        early_value().start()
        early_tangent().start()

    start_dispatch(0)
    arrived(0, owners(0, PART_A))
    project(*UNITS[0], True)
    arrived(0, owners(0, PART_B))
    passed_on(0).start()
    start_dispatch(1)
    project(*UNITS[1], True)
    project(*UNITS[2], True)
    arrive(1)
    start_dispatch(2)
    start_dispatch(3)
    project(*UNITS[3], True)
    for n, (j, unit) in enumerate(UNITS):
        last = n == len(UNITS) - 1
        expand(j, unit, UNITS[n + 2] if AHEAD <= n + 2 < len(UNITS) else None, send_early if last else None)
        if n < 2:
            arrive(n + 2)
        if n + 4 < len(UNITS):
            project(*UNITS[n + 4], False)
        if n == 3:
            give_back(0)
        if unit == OWN:
            give_back(j)
        if j == 3 and unit != OTHER:
            give_back(j, owners(j, unit), unit == PART_A)
        if (j, unit) == (3, OTHER):
            early()

    final = PLANES - 1
    near = pl.ds(pl.multiple_of(x_half * (WIDTH // 2), WIDTH // 2), WIDTH // 2)
    far = pl.ds(pl.multiple_of((1 - x_half) * (WIDTH // 2), WIDTH // 2), WIDTH // 2)
    late_backs = back(64, lambda line: (final, (line >> 4) & 1))
    second_backs = back(64, lambda line: (final, (line >> 5) & 1))
    returned(final, cuts(final)[0])

    def pair_sum(pair, i, cols):
        both = ret[final, 2 * pair, i, :, cols].astype(f32) + ret[final, 2 * pair + 1, i, :, cols].astype(f32)
        return both.astype(bf16)

    for pair in range(2):
        slot_value[x_half, pair] = pair_sum(pair, 0, slice(0, BLOCK))
    late_value().start()
    for pair in range(2):
        tangent_out[pair, :, : WIDTH // 2] = pair_sum(pair, 1, far)
        tangent_out[pair, :, WIDTH // 2 :] = pair_sum(pair, 1, slice(WIDTH, BLOCK))
    late_tangent().start()
    for pair in range(2):
        slot_tangent[x_half, pair, :, : WIDTH // 2] = pair_sum(pair, 1, near)
        slot_tangent[x_half, pair, :, WIDTH // 2 :] = pair_sum(pair, 1, slice(WIDTH, BLOCK))

    returned(final, cuts(final)[1])

    def late_second(f, _):
        cols = pl.ds(pl.multiple_of(f * PIECE, PIECE), PIECE)
        whole = ret[final, :, 2, :, cols].reshape(64, PIECE)
        extra = ret[final, :, 2, :, WIDTH:].reshape(64, PIECE)
        bown[:, cols] += picked(second_backs, whole, extra, f)
        return 0

    lax.fori_loop(0, FOLD, late_second, 0)

    def late_piece(f, _):
        cols = pl.ds(pl.multiple_of(f * PIECE, PIECE), PIECE)
        whole = slot_value[:, :, :, cols].reshape(64, PIECE)
        extra = slot_value[:, :, :, WIDTH:].reshape(64, PIECE)
        value = picked(late_backs, whole, extra, f)
        usum[:, cols] = value[:TOK] + value[TOK:]
        return 0

    def late_slope(f, _):
        cols = pl.ds(pl.multiple_of(f * PIECE, PIECE), PIECE)
        whole = slot_tangent[:, :, :, cols].reshape(64, PIECE)
        extra = slot_tangent[:, :, :, WIDTH // 2 :].reshape(64, PIECE)
        aown[x_half, :, cols] += picked(late_backs, whole, extra, x_half * 4 + f)
        return 0

    me = x_half * 2 + part
    lane = iota((16, 128), 1)

    def over(v):
        return jnp.sum(v, axis=-1, keepdims=True)

    def lay(values, laid):
        for i, value in values.items():
            laid = jnp.where(lane == i, value, laid)
        return laid

    def inner_value(block, _):
        at_ = pl.ds(pl.multiple_of(block * 16, 16), 16)
        u = tokens_ref[at_].astype(f32) + (pown[at_].astype(f32) + prec[at_].astype(f32)) + usum[at_]
        usum[at_] = u
        gain = gain_ref[...]
        heavy = gain * gain * u
        goal = gain * targets_ref[at_].astype(f32)
        stats = {}
        for k in range(2):
            b = bown[pl.ds(pl.multiple_of(k * TOK + block * 16, 16), 16)]
            stats[3 + k * 8 + 2] = over(u * b)
            stats[3 + k * 8 + 5] = over(heavy * b)
            stats[3 + k * 8 + 6] = over(goal * b)
        gain = gain_ref[:, near]
        u = usum[at_, near]
        heavy = gain * gain * u
        goal = gain * targets_ref[at_, near].astype(f32)
        stats[0] = over(u * u)
        stats[1] = over(heavy * u)
        stats[2] = over(goal * u)
        stat[me, at_] = lay(stats, jnp.zeros((16, 128), f32))
        return 0

    def inner_tangent(block, _):
        at_ = pl.ds(pl.multiple_of(block * 16, 16), 16)
        gain = gain_ref[:, near]
        u = usum[at_, near]
        heavy = gain * gain * u
        goal = gain * targets_ref[at_, near].astype(f32)
        stats = {}
        for k in range(2):
            own = pl.ds(pl.multiple_of(k * TOK + block * 16, 16), 16)
            a = aown[x_half, own] + arec[own].astype(f32)
            stats[3 + k * 8 + 0] = over(u * a)
            stats[3 + k * 8 + 1] = over(a * a)
            stats[3 + k * 8 + 3] = over(gain * gain * a * a)
            stats[3 + k * 8 + 4] = over(heavy * a)
            stats[3 + k * 8 + 7] = over(goal * a)
        stat[me, at_] = lay(stats, stat[me, at_])
        return 0

    early_value().wait_recv()
    late_value().wait_recv()
    lax.fori_loop(0, FOLD, late_piece, 0)
    lax.fori_loop(0, TOK // 16, inner_value, 0)
    early_tangent().wait_recv()
    late_tangent().wait_recv()
    lax.fori_loop(0, FOLD // 2, late_slope, 0)
    lax.fori_loop(0, TOK // 16, inner_tangent, 0)

    def stat_copy(i, who):
        return pltpu.make_async_remote_copy(
            src_ref=stat.at[me], dst_ref=stat.at[me], send_sem=st_send.at[i], recv_sem=st_recv.at[i], device_id=who
        )

    for i, who in enumerate((beside, across, diagonal)):
        stat_copy(i, who).start()
    for i, who in enumerate((beside, across, diagonal)):
        stat_copy(i, who).wait_recv()
    total = (stat[0] + stat[1]) + (stat[2] + stat[3])

    def column(i):
        return total[:, i : i + 1]

    inv_root = lax.rsqrt(column(0) / D + epsilon)
    weighted_uu = column(1)
    resid_u = inv_root * weighted_uu - column(2)
    sums = jnp.zeros((1, 128), f32)
    pairs = jnp.zeros((1, 128), f32)
    curves = []
    for k in range(2):
        m = [column(3 + k * 8 + i) for i in range(8)]
        curve = slot_curvature(
            inv_root, m[:5], weighted_uu, inv_root * m[5] - m[6], inv_root * m[4] - m[7], resid_u
        )
        curves.append(jnp.sum(jnp.where(eye_tok, curve, 0.0), axis=0, keepdims=True))
        member = ones_where(iota((TOK, 128), 1).astype(f32) == id_col[k])
        sums = sums + jnp.sum(member * curve, axis=0, keepdims=True)
        pairs = pairs + jnp.sum(member, axis=0, keepdims=True)
    row = iota((8, 128), 0)
    est_core[core] = jnp.where(row == 0, sums, jnp.where(row == 1, pairs, 0.0))
    core_copy = pltpu.make_async_remote_copy(
        src_ref=est_core.at[core], dst_ref=est_core.at[core], send_sem=c_send, recv_sem=c_recv, device_id=sibling
    )
    core_copy.start()
    core_copy.wait_recv()
    est_all[chip] = est_core[0] + est_core[1]

    def all_copy(delta):
        return pltpu.make_async_remote_copy(
            src_ref=est_all.at[chip], dst_ref=est_all.at[chip], send_sem=a_send.at[delta], recv_sem=a_recv.at[delta],
            device_id=at((chip + delta) % 16),
        )

    def start_all(delta, _):
        all_copy(delta).start()
        return 0

    lax.fori_loop(1, 16, start_all, 0)
    for block in range(TOK // 16):
        at_ = slice(block * 16, (block + 1) * 16)
        normed_ref[at_] = (gain_ref[...] * usum[at_] * inv_root[at_]).astype(bf16)

    for j in range(PLANES):
        end_dispatch(j)
        passed_on(j).wait_send()
        to_sibling(j).wait_send()

        def gone(q, _):
            for cut in cuts(j):
                mine, _, there = give(j, q, cut)

                @pl.when(jnp.logical_not(mine))
                def _():
                    there.wait_send()

            return 0

        lax.fori_loop(0, 4, gone, 0)
    for j, unit in UNITS:
        for i in range(3):
            exchange(j, unit, i).wait_send()
    for copy in (early_value(), early_tangent(), late_value(), late_tangent()):
        copy.wait_send()
    for i, who in enumerate((beside, across, diagonal)):
        stat_copy(i, who).wait_send()
    core_copy.wait_send()

    def end_all(delta, _):
        all_copy(delta).wait()
        return 0

    lax.fori_loop(1, 16, end_all, 0)
    mean = jnp.sum(est_all[...], axis=0)
    small_ref[0:2, 0:TOK] = jnp.concatenate(curves, axis=0)
    small_ref[2:3, :] = mean[0:1] / jnp.maximum(mean[1:2], 1.0)


def deliver(normed_in, small_in, normed_ref, curv_ref, est_ref):
    normed_ref[...] = normed_in[...]
    curv_ref[...] = small_in[0:2, 0:TOK]
    est_ref[...] = small_in[2:3, 0:EXPERTS]


def on_device(tokens, targets, norm_gain, expert_ids, gate_prob, w_gate, gate_probe, w_up, w_down):
    vmem = pl.BlockSpec(memory_space=pltpu.VMEM)
    anywhere = pl.BlockSpec(memory_space=pl.ANY)
    dma = pltpu.SemaphoreType.DMA
    normed, small = pl.pallas_call(
        kernel,
        out_shape=(
            jax.ShapeDtypeStruct((TOK, WIDTH), bf16),
            jax.ShapeDtypeStruct((8, 128), f32),
        ),
        in_specs=[vmem] * 5 + [anywhere] * 4,
        out_specs=(vmem, vmem),
        scratch_shapes=[
            pltpu.VMEM((6, WIDTH, HALF), bf16),
            pltpu.VMEM((HIDDEN, WIDTH), bf16),
            pltpu.VMEM((EXPERTS, MAIN, BLOCK), bf16),
            pltpu.VMEM((PLANES, 2, 4, MAIN, BLOCK), bf16),
            pltpu.VMEM((ROWS, WIDTH), bf16),
            pltpu.VMEM((PLANES, 3, ROWS, HIDDEN), bf16),
            pltpu.VMEM((PLANES, 3, ROWS, HIDDEN), bf16),
            pltpu.VMEM((3 * ROWS, HIDDEN), bf16),
            pltpu.VMEM((3, 128, PIECE), bf16),
            pltpu.VMEM((PLANES, 2, 4, 3, MAIN, BLOCK), bf16),
            pltpu.VMEM((PLANES, 4, 3, MAIN, BLOCK), bf16),
            pltpu.VMEM((PLANES, 4, 3, MAIN, BLOCK), bf16),
            pltpu.VMEM((TOK, WIDTH), bf16),
            pltpu.VMEM((TOK, WIDTH), bf16),
            pltpu.VMEM((2, 2 * TOK, WIDTH // 2), f32),
            pltpu.VMEM((2, 2 * TOK, WIDTH // 2), bf16),
            pltpu.VMEM((2 * TOK, WIDTH // 2), bf16),
            pltpu.VMEM((2 * TOK, WIDTH), f32),
            pltpu.VMEM((TOK, WIDTH), f32),
            pltpu.VMEM((2, 2, MAIN, BLOCK), bf16),
            pltpu.VMEM((2, 2, MAIN, WIDTH // 2 + PIECE), bf16),
            pltpu.VMEM((2, MAIN, WIDTH // 2 + PIECE), bf16),
            pltpu.VMEM((4, TOK, 128), f32),
            pltpu.VMEM((2, 8, 128), f32),
            pltpu.VMEM((16, 8, 128), f32),
            dma((7,)),
            dma((PLANES, 4)), dma((PLANES, 4)),
            dma((PLANES,)), dma((PLANES,)),
            dma((PLANES, 3, 3)), dma((PLANES, 3, 3)),
            dma((PLANES,)), dma((PLANES,)),
            dma((PLANES + 1, 4)), dma((PLANES + 1, 4)),
            dma((4,)), dma((4,)),
            dma((3,)), dma((3,)),
            dma, dma,
            dma((16,)), dma((16,)),
        ],
        compiler_params=pltpu.CompilerParams(
            collective_id=0, has_side_effects=True, vmem_limit_bytes=60 * 1024 * 1024
        ),
    )(
        expert_ids.T,
        gate_prob.T,
        norm_gain.reshape(1, WIDTH),
        tokens,
        targets,
        w_gate,
        gate_probe,
        w_up,
        w_down,
    )
    normed, curvature, estimate = pl.pallas_call(
        deliver,
        out_shape=(
            jax.ShapeDtypeStruct((TOK, WIDTH), bf16),
            jax.ShapeDtypeStruct((2, TOK), f32),
            jax.ShapeDtypeStruct((1, EXPERTS), f32),
        ),
        in_specs=[vmem, vmem],
        out_specs=(vmem, vmem, vmem),
    )(normed, small)
    return normed, curvature.T, estimate.reshape(EXPERTS)


def solution(mesh):
    return jax.shard_map(
        on_device,
        mesh=mesh,
        in_specs=(
            P("dp", "tensor"),
            P("dp", "tensor"),
            P("tensor"),
            P("dp", None),
            P("dp", None),
            P("tensor", ("dp", "expert")),
            P("tensor", ("dp", "expert")),
            P("tensor", ("dp", "expert")),
            P(("dp", "expert"), "tensor"),
        ),
        out_specs=(P("dp", "tensor"), P("dp", None), P()),
        check_vma=False,
    )
```
